256 devices in a mesh: coarse: 32 (over y, x, core), leaf: 8 (over z).
Axes of the slice: x: 4, y: 4, z: 8, core: 2. Of those that a mesh axis runs over, the one named last changes fastest.
Arguments:
- vectors: bfloat16 [64, 1048576], P(None, ('coarse', 'leaf')), may hold values from -6 to 6
- leaf_basis: bfloat16 [32, 1048576], P(None, ('coarse', 'leaf')), may hold values from -0.75 to 0.75
- near_blocks: bfloat16 [12, 64, 1048576], P(None, None, ('coarse', 'leaf')), may hold values from -0.21875 to 0.21875
- near_index: int32 [12, 16384], P(None, ('coarse', 'leaf')), may hold values from 0 to 16383, as said below
- leaf_transfer: bfloat16 [32, 32, 16384], P(None, None, ('coarse', 'leaf')), may hold values from -0.75 to 0.75
- node_transfer: bfloat16 [32, 32, 2048], P(None, None, ('coarse', 'leaf')), may hold values from -0.75 to 0.75
- device_transfer: bfloat16 [32, 32, 256], P(None, None, ('coarse', 'leaf')), may hold values from -0.75 to 0.75
- leaf_lists: int32 [16, 16384], P(None, ('coarse', 'leaf')), may hold values from 0 to 16383, as said below
- leaf_coupling: bfloat16 [16, 32, 32, 16384], P(None, None, None, ('coarse', 'leaf')), may hold values from -0.25 to 0.25
- node_lists: int32 [16, 2048], P(None, ('coarse', 'leaf')), may hold values from 0 to 2047, as said below
- node_coupling: bfloat16 [16, 32, 32, 2048], P(None, None, None, ('coarse', 'leaf')), may hold values from -0.25 to 0.25
- device_lists: int32 [16, 256], P(None, ('coarse', 'leaf')), may hold values from 0 to 255
- device_coupling: bfloat16 [16, 32, 32, 256], P(None, None, None, ('coarse', 'leaf')), may hold values from -0.25 to 0.25
- group_lists: int32 [8, 32], P(None, 'coarse'), may hold values from 0 to 31
- group_coupling: bfloat16 [8, 32, 32, 32], P(None, None, None, 'coarse'), may hold values from -0.375 to 0.375
Outputs:
- product: bfloat16 [64, 1048576], P(None, ('coarse', 'leaf'))
The draws below stay inside these ranges and needn't reach their ends.
Inputs may be any that keep to these rules, and one draw needn't show every extreme that they name: `near_index`: leaves sit on a grid of 128 x 32 x 4. Device node b (b = x block * 8 + y block) holds the 4 x 4 x 4 leaves of its blocks; within it, node m = (i * 2 + j) * 2 + k is the node at node position (2 x block + i, 2 y block + j, k), and its child c = 4 a + 2 b + e the leaf at twice that position plus (a, b, e). Each entry names a leaf whose position differs from its column's leaf by at most one in each direction; slot 0 by one in every direction (reflected at the grid's faces). `leaf_lists`: positions as for near_index; each entry names a leaf not adjacent to its column's leaf whose parent node is the parent of that leaf or adjacent to it; entries of a column may repeat where the grid's faces leave fewer than 16 such leaves. `node_lists`: node positions as for near_index; each entry names a node not adjacent to its column's node whose position halved (rounded down) differs from the column node's halved position by at most one in each direction; entries may repeat near the grid's faces.
All inputs are finite; a program needn't handle non-finite values.
Results may differ from the reference program's by a relative error of at most 0.017.
Values may be sent and summed in bfloat16 or wider, within the bound.
No kernel may reach another device: no remote copies, remote signals or barrier semaphores. Data moves between devices by JAX's collectives and lax.ppermute only.
A program may use at most 192 MiB of HBM per device.

```python
from functools import partial
import jax
import jax.numpy as jnp
import numpy as np
from jax import lax

LEAF = 64
RANK = 32
VECS = 64
BZ = 4
NEAR = 12
INTER_LEAF = 16
INTER_NODE = 16
INTER_DEVICE = 16
INTER_GROUP = 8
LEAVES_DEV = 64
NODE_DEV = 8
GRID_X = 128
GRID_Y = 32
DEVICE_NODES = 256
GROUPS = 32
LEAVES = 16384
NODES = 2048
POINTS = 1048576
N_LEAF = 8


unit_steps = np.array([-1, 0, 1], dtype=np.int32)


child_steps = np.array([0, 1], dtype=np.int32)


near_offsets = np.stack(np.meshgrid(unit_steps, unit_steps, unit_steps, indexing='ij'), axis=-1).reshape(27, 3).astype(np.int32)


far_offsets = np.stack(np.meshgrid(unit_steps, unit_steps, unit_steps, child_steps, child_steps, child_steps, indexing='ij'), axis=-1).reshape(216, 6).astype(np.int32)


def node_place(numbers, half):
    block = numbers // (4 * half)
    rest = numbers % (4 * half)
    place_x = 2 * (block // N_LEAF) + rest // (2 * half)
    place_y = 2 * (block % N_LEAF) + rest // half % 2
    return (place_x, place_y, rest % half)


def node_number(place_x, place_y, place_z, half):
    block = place_x // 2 * N_LEAF + place_y // 2
    return block * (4 * half) + (place_x % 2 * 2 + place_y % 2) * half + place_z


def leaf_place(numbers):
    node_x, node_y, node_z = node_place(numbers // 8, BZ // 2)
    child = numbers % 8
    return (2 * node_x + child // 4, 2 * node_y + child // 2 % 2, 2 * node_z + child % 2)


def leaf_number(place_x, place_y, place_z):
    parent = node_number(place_x // 2, place_y // 2, place_z // 2, BZ // 2)
    return parent * 8 + place_x % 2 * 4 + place_y % 2 * 2 + place_z % 2


def far_draw(key, count, places, extent, numbering):
    table = jnp.asarray(far_offsets)
    base = jnp.stack(places, axis=-1)
    total = base.shape[0]
    target = 2 * (base[:, None, :] // 2 + table[None, :, :3]) + table[None, :, 3:]
    inside = jnp.all((target >= 0) & (target < extent[None, None, :]), axis=-1)
    adjacent = jnp.all(jnp.abs(target - base[:, None, :]) <= 1, axis=-1)
    valid = inside & jnp.logical_not(adjacent)
    scores = jax.random.randint(key, (total, 216), 0, 1 << 20, dtype=jnp.int32) * 256 + jnp.arange(216, dtype=jnp.int32)[None, :]
    scores = scores + jnp.where(valid, 0, 1 << 29).astype(jnp.int32)
    order = jnp.argsort(scores, axis=1).astype(jnp.int32)
    live = jnp.sum(valid.astype(jnp.int32), axis=1)
    slots = jnp.arange(count, dtype=jnp.int32)[None, :] % live[:, None]
    picked = jnp.take_along_axis(order, slots, axis=1)
    chosen = jnp.take_along_axis(target, picked[:, :, None], axis=1)
    numbers = numbering(chosen[:, :, 0], chosen[:, :, 1], chosen[:, :, 2])
    return jnp.transpose(numbers).astype(jnp.int32)


def draw_near_index(key, part):
    key = jax.random.fold_in(key, 1)
    place_x, place_y, place_z = leaf_place(jnp.arange(LEAVES, dtype=jnp.int32))
    base = jnp.stack([place_x, place_y, place_z], axis=-1)[:, None, :]
    extent = jnp.array([GRID_X, GRID_Y, BZ], dtype=jnp.int32)
    scores = jax.random.randint(key, (LEAVES, 27), 0, 1 << 20, dtype=jnp.int32) * 32 + jnp.arange(27, dtype=jnp.int32)[None, :]
    order = jnp.argsort(scores, axis=1)[:, :NEAR - 1]
    chosen = jnp.asarray(near_offsets)[order]
    corner = 2 * jax.random.randint(jax.random.fold_in(key, 5), (LEAVES, 1, 3), 0, 2, dtype=jnp.int32) - 1
    offsets = jnp.concatenate([corner, chosen], axis=1)
    target = base + offsets
    inside = (target >= 0) & (target < extent[None, None, :])
    target = jnp.where(inside, target, base - offsets)
    numbers = leaf_number(target[:, :, 0], target[:, :, 1], target[:, :, 2])
    return jnp.transpose(numbers).astype(jnp.int32)


def draw_leaf_lists(key, part):
    key = jax.random.fold_in(key, 2)
    places = leaf_place(jnp.arange(LEAVES, dtype=jnp.int32))
    extent = jnp.array([GRID_X, GRID_Y, BZ], dtype=jnp.int32)
    return far_draw(key, INTER_LEAF, places, extent, leaf_number)


def draw_node_lists(key, part):
    key = jax.random.fold_in(key, 3)
    places = node_place(jnp.arange(NODES, dtype=jnp.int32), BZ // 2)
    extent = jnp.array([GRID_X // 2, GRID_Y // 2, BZ // 2], dtype=jnp.int32)
    return far_draw(key, INTER_NODE, places, extent, partial(node_number, half=BZ // 2))


def touch_ends(entries, key, low, top_value):
    longest = entries.shape.index(max(entries.shape))
    spots = []
    for shift in (0, 1):
        where = [jax.random.randint(jax.random.fold_in(key, axis), (), 0, length) for axis, length in enumerate(entries.shape)]
        where[longest] = (where[longest] + shift) % entries.shape[longest]
        spots.append(tuple(where))
    return entries.at[spots[0]].set(low).at[spots[1]].set(top_value)


def block_scale(stream_key, shape, split, smallest, largest):
    factor_of = 1.0
    for dim, blocks in split:
        draws = jax.random.uniform(jax.random.fold_in(jax.random.fold_in(stream_key, 6), dim), (blocks,), jnp.float32, smallest / len(split), largest / len(split))
        factor_of = factor_of * jnp.repeat(jnp.exp(draws), shape[dim] // blocks).reshape((-1,) + (1,) * (len(shape) - 1 - dim))
    return factor_of


def normal_values(own_key, shape, scale, reach, pieces=(), kind=jnp.bfloat16):
    drawn = jax.random.normal(own_key, shape, jnp.float32) * scale
    if len(pieces) > 0:
        drawn = block_scale(own_key, shape, pieces, -0.22, 0.18) * drawn
    return jnp.clip(drawn, min=-reach, max=reach).astype(kind)


def setup_inputs(seed: int = 0) -> dict:
    streams_of = jax.random.split(jax.random.key(seed), 16)
    vectors = normal_values(streams_of[0], (VECS, POINTS), 1.0, 6.0, ((1, 256),))
    leaf_basis = normal_values(streams_of[1], (RANK, POINTS), LEAF ** -0.5, 0.75, ((1, 256),))
    near_blocks = normal_values(streams_of[2], (NEAR, LEAF, POINTS), (NEAR * LEAF) ** -0.5, 0.21875, ((2, 256),))
    near_index = draw_near_index(jax.random.fold_in(streams_of[15], 71), 0)
    leaf_transfer = normal_values(streams_of[4], (RANK, RANK, LEAVES), (2 * RANK) ** -0.5, 0.75, ((2, 256),))
    node_transfer = normal_values(streams_of[5], (RANK, RANK, NODES), (2 * RANK) ** -0.5, 0.75, ((2, 256),))
    device_transfer = normal_values(streams_of[6], (RANK, RANK, DEVICE_NODES), (2 * RANK) ** -0.5, 0.75, ((2, 256),))
    leaf_lists = draw_leaf_lists(jax.random.fold_in(streams_of[15], 71), 0)
    leaf_coupling = normal_values(streams_of[8], (INTER_LEAF, RANK, RANK, LEAVES), (INTER_LEAF * RANK) ** -0.5, 0.25, ((3, 256),))
    node_lists = draw_node_lists(jax.random.fold_in(streams_of[15], 71), 0)
    node_coupling = normal_values(streams_of[10], (INTER_NODE, RANK, RANK, NODES), (INTER_NODE * RANK) ** -0.5, 0.25, ((3, 256),))
    device_lists = touch_ends(jax.random.randint(streams_of[11], (INTER_DEVICE, DEVICE_NODES), 0, DEVICE_NODES), jax.random.fold_in(streams_of[11], 1), 0, DEVICE_NODES - 1).astype(jnp.int32)
    device_coupling = normal_values(streams_of[12], (INTER_DEVICE, RANK, RANK, DEVICE_NODES), (INTER_DEVICE * RANK) ** -0.5, 0.25, ((3, 256),))
    group_lists = touch_ends(jax.random.randint(streams_of[13], (INTER_GROUP, GROUPS), 0, GROUPS), jax.random.fold_in(streams_of[13], 1), 0, GROUPS - 1).astype(jnp.int32)
    group_coupling = normal_values(streams_of[14], (INTER_GROUP, RANK, RANK, GROUPS), (INTER_GROUP * RANK) ** -0.5, 0.375, ((3, 32),))
    return {"vectors": vectors, "leaf_basis": leaf_basis, "near_blocks": near_blocks, "near_index": near_index, "leaf_transfer": leaf_transfer, "node_transfer": node_transfer, "device_transfer": device_transfer, "leaf_lists": leaf_lists, "leaf_coupling": leaf_coupling, "node_lists": node_lists, "node_coupling": node_coupling, "device_lists": device_lists, "device_coupling": device_coupling, "group_lists": group_lists, "group_coupling": group_coupling}


def coupling(coefs, index, blocks, parts):
    width = index.shape[1] // parts

    def one_part(number):
        start = number * width
        chosen = lax.dynamic_slice_in_dim(index, start, width, 1)
        local_blocks = lax.dynamic_slice_in_dim(blocks, start, width, 3)
        picked = jnp.take(coefs, chosen, axis=2).astype(jnp.float32)
        return jnp.einsum('vksn,sjkn->nvj', picked, local_blocks.astype(jnp.float32))

    result = lax.map(one_part, jnp.arange(parts, dtype=jnp.int32))
    result = result.reshape(parts * width, result.shape[2], result.shape[3])
    return jnp.transpose(result, (1, 2, 0))


def near_field(vectors, near_blocks, near_index):
    grouped = vectors.reshape(VECS, LEAVES, LEAF)

    def one_part(number):
        start = number * LEAVES_DEV
        chosen = lax.dynamic_slice_in_dim(near_index, start, LEAVES_DEV, 1)
        blocks = lax.dynamic_slice_in_dim(near_blocks, start * LEAF, LEAVES_DEV * LEAF, 2)
        blocks = blocks.reshape(NEAR, LEAF, LEAVES_DEV, LEAF).astype(jnp.float32)
        picked = jnp.take(grouped, chosen, axis=1).astype(jnp.float32)
        return jnp.einsum('vslq,sqlp->lvp', picked, blocks)

    result = lax.map(one_part, jnp.arange(DEVICE_NODES, dtype=jnp.int32))
    result = result.reshape(LEAVES, VECS, LEAF)
    return jnp.transpose(result, (1, 0, 2)).reshape(VECS, POINTS)


def reference(vectors, leaf_basis, near_blocks, near_index, leaf_transfer, node_transfer, device_transfer, leaf_lists, leaf_coupling, node_lists, node_coupling, device_lists, device_coupling, group_lists, group_coupling):
    basis = leaf_basis.reshape(RANK, LEAVES, LEAF).astype(jnp.float32)
    leaf_coefs = jnp.einsum('vlp,klp->vkl', vectors.reshape(VECS, LEAVES, LEAF).astype(jnp.float32), basis).astype(jnp.bfloat16)
    node_coefs = jnp.einsum('vkni,kjni->vjn', leaf_coefs.reshape(VECS, RANK, NODES, 8).astype(jnp.float32), leaf_transfer.reshape(RANK, RANK, NODES, 8).astype(jnp.float32)).astype(jnp.bfloat16)
    device_coefs = jnp.einsum('vkdi,kjdi->vjd', node_coefs.reshape(VECS, RANK, DEVICE_NODES, NODE_DEV).astype(jnp.float32), node_transfer.reshape(RANK, RANK, DEVICE_NODES, NODE_DEV).astype(jnp.float32)).astype(jnp.bfloat16)
    device_terms = jnp.einsum('vkd,kjd->vjd', device_coefs.astype(jnp.float32), device_transfer.astype(jnp.float32)).astype(jnp.bfloat16)
    group_coefs = jnp.sum(device_terms.astype(jnp.float32).reshape(VECS, RANK, GROUPS, DEVICE_NODES // GROUPS), axis=3).astype(jnp.bfloat16)
    group_field = coupling(group_coefs, group_lists, group_coupling, 1).astype(jnp.bfloat16)
    parent_group = jnp.repeat(group_field, DEVICE_NODES // GROUPS, axis=2).astype(jnp.float32)
    device_field = (coupling(device_coefs, device_lists, device_coupling, 1) + jnp.einsum('vjd,kjd->vkd', parent_group, device_transfer.astype(jnp.float32))).astype(jnp.bfloat16)
    parent_device = jnp.repeat(device_field, NODE_DEV, axis=2).astype(jnp.float32)
    node_field = (coupling(node_coefs, node_lists, node_coupling, DEVICE_NODES) + jnp.einsum('vjn,kjn->vkn', parent_device, node_transfer.astype(jnp.float32))).astype(jnp.bfloat16)
    parent_node = jnp.repeat(node_field, 8, axis=2).astype(jnp.float32)
    leaf_field = (coupling(leaf_coefs, leaf_lists, leaf_coupling, DEVICE_NODES) + jnp.einsum('vjl,kjl->vkl', parent_node, leaf_transfer.astype(jnp.float32))).astype(jnp.bfloat16)
    far_part = jnp.einsum('vkl,klp->vlp', leaf_field.astype(jnp.float32), basis).reshape(VECS, POINTS)
    return (near_field(vectors, near_blocks, near_index) + far_part).astype(jnp.bfloat16)
```

```python
import jax
import jax.numpy as jnp
from jax import lax
from jax.experimental import pallas as pl
from jax.experimental.pallas import tpu as pltpu
from jax.sharding import PartitionSpec as P

BF = jnp.bfloat16
F32 = jnp.float32
V1, C1, N1 = 512, 512, 128
V2, C2, N2 = 768, 1024, 384
ROWS1 = V1 + C1 + N1
ROWS2 = V2 + C2 + N2
TAB = 144
MB = 1024 * 1024


def dot(a, b, ca, cb):
    return lax.dot_general(a, b, (((ca,), (cb,)), ((), ())), preferred_element_type=F32)


def copies(pairs, sems):
    started = [pltpu.make_async_copy(src, dst, sems.at[i]) for i, (src, dst) in enumerate(pairs)]
    for c in started:
        c.start()
    return started


def eye(n):
    rows = lax.broadcasted_iota(jnp.int32, (n, n), 0)
    cols = lax.broadcasted_iota(jnp.int32, (n, n), 1)
    return jnp.where(rows == cols, 1.0, 0.0).astype(BF)


def diagonal_mask():
    rows = lax.broadcasted_iota(jnp.int32, (128, 256), 0)
    cols = lax.broadcasted_iota(jnp.int32, (128, 256), 1)
    return jnp.where((rows >> 5) == (cols >> 6), 1.0, 0.0).astype(BF)


def low_lanes(rows):
    return lax.broadcasted_iota(jnp.int32, (rows, 128), 1) < 64


def node_parts(node):
    block, rest = node >> 3, node & 7
    return 2 * (block >> 3) + (rest >> 2), 2 * (block & 7) + ((rest >> 1) & 1), rest & 1


def up_kernel(
    v_hbm, b_hbm, lt_hbm, nt_hbm, dt_hbm, pay, cown, nown, up, dn, tl, fup, fdn,
    ct, tls, ncs, lt, v, b, nt, dt, sems,
):
    loads = copies(
        [
            (lt_hbm, lt), (v_hbm, v), (b_hbm, b), (nt_hbm, nt), (dt_hbm, dt),
        ],
        sems,
    )
    ident = eye(64)
    loads[0].wait()
    for k in range(32):
        tls[pl.ds(k, 64, stride=32), :] = dot(
            ident, jnp.concatenate([lt[k], jnp.zeros((96, 64), BF)], axis=0), 1, 1
        )
    tl[...] = tls[...].astype(BF)
    for c in loads[1:]:
        c.wait()
    mask = diagonal_mask()
    for g in range(16):
        lanes = slice(g * 256, (g + 1) * 256)
        bg = b[:, lanes]
        bd = jnp.concatenate([bg, bg, bg, bg], axis=0) * mask
        c = dot(bd, v[:, lanes], 1, 1)
        ct[g * 128:(g + 1) * 128, :] = c.astype(BF)
        for h in range(2):
            pair = jnp.concatenate([c[h * 64:h * 64 + 32], c[h * 64 + 32:h * 64 + 64]], axis=1)
            cown[(2 * g + h) * 32:(2 * g + h + 1) * 32, :] = pair.astype(BF)
    for m in range(4):
        parts = []
        for n in (2 * m, 2 * m + 1):
            rows = slice(n * 256, (n + 1) * 256)
            nc = dot(tl[rows, :32], ct[rows, :], 0, 0)
            parts.append(nc)
            wide = jnp.concatenate([nc, nc], axis=1)
            ncs[pl.ds(n, 32, stride=8), :] = wide.astype(BF).astype(F32)
        nown[m * 32:(m + 1) * 32, :] = jnp.concatenate(parts, axis=1).astype(BF)
    dc = dot(nt[...], ncs[...].astype(BF), 0, 0)
    terms = dot(dt[...], dc.astype(BF), 0, 0)
    message = jnp.where(low_lanes(32), dc, terms).astype(BF)
    for z in range(8):
        pay[z] = message
    for j in range(2):
        for k in range(2):
            for bb in range(2):
                at = ((2 * j + k) * 2 + bb) * 64
                first = ((2 * j + k) * 8 + 2 * bb) * 64
                dn[at:at + 64, :] = v[:, first:first + 128]
                first += 36 * 64
                up[at:at + 64, :] = v[:, first:first + 128]
    for i in range(2):
        for a in range(2):
            for k in range(2):
                at = ((i * 2 + a) * 2 + k) * 64
                first = ((i * 4 + k) * 8 + 4 * a) * 64
                fdn[at:at + 64, :] = v[:, first:first + 128]
                first += 18 * 64
                fup[at:at + 64, :] = v[:, first:first + 128]
    dn[V1:V1 + C1, :] = cown[0:512, :]
    up[V1:V1 + C1, :] = cown[512:1024, :]
    dn[V1 + C1:, :] = nown[...]
    up[V1 + C1:, :] = nown[...]


def pack_kernel(fup, fdn, cown, nown, bef, aft, up, dn, sems):
    moves = []
    for out, face, j in ((up, fup, 1), (dn, fdn, 0)):
        rows = [(face, 0, 512)]
        for side in (bef, aft):
            rows += [(side, ((2 * j + k) * 2 + j) * 64, 64) for k in range(2)]
        rows += [(cown, (i * 2 + j) * 256, 256) for i in range(2)]
        rows += [(side, V1 + j * 256, 256) for side in (bef, aft)]
        rows += [(nown, 0, 128), (bef, V1 + C1, 128), (aft, V1 + C1, 128)]
        at = 0
        for side, first, count in rows:
            moves.append((side.at[pl.ds(first, count)], out.at[pl.ds(at, count)]))
            at += count
    for c in copies(moves, sems):
        c.wait()


def group_kernel(r, after, y):
    low = low_lanes(32)
    total = jnp.zeros((32, 128), F32)
    for m in range(4):
        lo, hi = r[2 * m].astype(F32), r[2 * m + 1].astype(F32)
        total = total + lo + hi
        y[m * 32:(m + 1) * 32, :] = jnp.where(low, lo, pltpu.roll(hi, 64, 1)).astype(BF)
    swapped = pltpu.roll(total, 64, 1)
    y[128:144, :] = jnp.where(low_lanes(16), swapped[0:16], total[16:32]).astype(BF)


def prep_kernel(
    near_in, leaf_in, node_in, s_hbm, sn_hbm, sd_hbm, sg_hbm,
    zl, zn, zd, zg, near_ix, leaf_ix, node_ix, zs, ns, s, sn, sd, sg, sems,
):
    loads = copies(
        [(s_hbm.at[:, pl.ds(8 * q, 8)], s.at[:, pl.ds(8 * q, 8)]) for q in range(4)]
        + [(sn_hbm, sn), (sd_hbm, sd), (sg_hbm, sg)],
        sems,
    )
    cp, lp = lax.axis_index("coarse"), lax.axis_index("leaf")
    num = near_in[...]
    px, py, pz = node_parts(num >> 3)
    lx = 2 * px + ((num >> 2) & 1) - 4 * cp + 1
    ly = 2 * py + ((num >> 1) & 1) - 4 * lp + 1
    near_ix[...] = jnp.clip((lx * 6 + ly) * 4 + 2 * pz + (num & 1), 0, 143)
    num = leaf_in[...]
    px, py, pz = node_parts(num >> 3)
    at = ((px - 2 * cp + 1) * 4 + (py - 2 * lp + 1)) * 2 + pz
    leaf_ix[...] = jnp.clip(at * 8 + (num & 7), 0, 255)
    px, py, pz = node_parts(node_in[...])
    at = ((px - 2 * cp + 2) * 6 + (py - 2 * lp + 2)) * 2 + pz
    node_ix[...] = jnp.clip(at, 0, 71)
    ident = eye(64)
    for j in range(32):
        if j % 8 == 0:
            loads[j // 8].wait()
        t = dot(ident, s[:, j].reshape(512, 64), 1, 1)
        for q in range(4):
            zs[q, pl.ds(j, 64, stride=32), :] = t[:, q * 128:(q + 1) * 128]
    for c in loads[4:]:
        c.wait()
    for q in range(4):
        zl[:, q * 128:(q + 1) * 128] = zs[q].astype(BF)
        parts = [sn[4 * q + i].astype(F32).reshape(256, 32) for i in range(4)]
        ns[...] = jnp.concatenate(parts, axis=1)
        for n in range(8):
            zn[n * 32:(n + 1) * 32, q * 128:(q + 1) * 128] = ns[pl.ds(n, 32, stride=8), :].astype(BF)
        parts = [sd[4 * q + i].astype(F32) for i in range(4)]
        zd[:, q * 128:(q + 1) * 128] = jnp.concatenate(parts, axis=1).astype(BF)
    for q in range(2):
        parts = [sg[4 * q + i].astype(F32) for i in range(4)]
        zg[:, q * 128:(q + 1) * 128] = jnp.concatenate(parts, axis=1).astype(BF)


def near_kernel(ix_any, v, bef, aft, lb, la, blocks_hbm, out, low, high, picked, ix, blocks, sems):
    loads = copies(
        [(ix_any, ix)]
        + [(blocks_hbm.at[:, pl.ds(512 * t, 512)], blocks.at[t]) for t in range(8)],
        sems,
    )
    mask = low_lanes(64)

    def table():
        def put(wx, wy, k, x):
            at = (wx * 6 + wy) * 4 + 2 * k
            x = x.astype(F32)
            swapped = pltpu.roll(x, 64, 1)
            low[at] = jnp.where(mask, x, 0.0).astype(BF)
            high[at] = jnp.where(mask, 0.0, swapped).astype(BF)
            low[at + 1] = jnp.where(mask, swapped, 0.0).astype(BF)
            high[at + 1] = jnp.where(mask, 0.0, x).astype(BF)

        for i in range(2):
            for j in range(2):
                for k in range(2):
                    for a in range(2):
                        for bb in range(2):
                            first = (((i * 2 + j) * 2 + k) * 8 + 4 * a + 2 * bb) * 64
                            put(1 + 2 * i + a, 1 + 2 * j + bb, k, v[:, first:first + 128])
        for side, wx in ((bef, 0), (aft, 5)):
            for j in range(2):
                for k in range(2):
                    for bb in range(2):
                        first = ((2 * j + k) * 2 + bb) * 64
                        put(wx, 1 + 2 * j + bb, k, side[first:first + 64, :])
        for side, wy in ((lb, 0), (la, 5)):
            for i in range(2):
                for a in range(2):
                    for k in range(2):
                        first = ((i * 2 + a) * 2 + k) * 64
                        put(1 + 2 * i + a, wy, k, side[first:first + 64, :])
            for wx, base in ((0, 8), (5, 10)):
                for k in range(2):
                    first = (base + k) * 64
                    put(wx, wy, k, side[first:first + 64, :])

    table()
    loads[0].wait()

    def chunk(t, carry):
        pltpu.make_async_copy(
            blocks_hbm.at[:, pl.ds(pl.multiple_of(512 * t, 512), 512)], blocks.at[t], sems.at[t + 1]
        ).wait()
        for q in range(4):
            for i in range(2):
                leaf = t * 8 + 2 * q + i
                for sp in range(6):
                    picked[q, i * 64:(i + 1) * 64, sp * 128:(sp + 1) * 128] = (
                        low[ix[2 * sp, leaf]] + high[ix[2 * sp + 1, leaf]]
                    )
            r = dot(picked[q], blocks[t, :, q * 128:(q + 1) * 128], 1, 0)
            lanes = pl.ds(pl.multiple_of(t * 512 + q * 128, 128), 128)
            out[:, lanes] = jnp.where(mask, r[:64], r[64:])
        return carry

    lax.fori_loop(0, 8, chunk, 0)


def far_kernel(
    li_any, mi_any, cown, nown, bef, aft, lb, la, zl, zn, far, nfar, cw, nw, li, mi, sems
):
    loads = copies([(li_any, li), (mi_any, mi)], sems)

    def put_leaves(nwx, nwy, k, side, first):
        for p in range(4):
            x = side[first + p * 32:first + (p + 1) * 32, :]
            at = ((nwx * 4 + nwy) * 2 + k) * 8 + 2 * p
            cw[at] = x
            cw[at + 1] = pltpu.roll(x.astype(F32), 64, 1).astype(BF)

    def put_nodes(nwx, nwy, side, first):
        x = side[first:first + 32, :]
        at = (nwx * 6 + nwy) * 2
        nw[at] = x
        nw[at + 1] = pltpu.roll(x.astype(F32), 64, 1).astype(BF)

    for i in range(2):
        for j in range(2):
            put_nodes(2 + i, 2 + j, nown, (i * 2 + j) * 32)
            put_nodes(i, 2 + j, bef, V1 + C1 + (i * 2 + j) * 32)
            put_nodes(4 + i, 2 + j, aft, V1 + C1 + (i * 2 + j) * 32)
            for side, base in ((lb, 0), (la, 4)):
                first = V2 + C2 + (i * 2 + j) * 32
                put_nodes(2 + i, base + j, side, first)
                put_nodes(i, base + j, side, first + 128)
                put_nodes(4 + i, base + j, side, first + 256)
            for k in range(2):
                put_leaves(1 + i, 1 + j, k, cown, ((i * 2 + j) * 2 + k) * 128)
    for j in range(2):
        for k in range(2):
            put_leaves(0, 1 + j, k, bef, V1 + (2 * j + k) * 128)
            put_leaves(3, 1 + j, k, aft, V1 + (2 * j + k) * 128)
    for side, nwy in ((lb, 0), (la, 3)):
        for k in range(2):
            for i in range(2):
                put_leaves(1 + i, nwy, k, side, V2 + (2 * i + k) * 128)
            put_leaves(0, nwy, k, side, V2 + 512 + k * 128)
            put_leaves(3, nwy, k, side, V2 + 768 + k * 128)

    for c in loads:
        c.wait()
    for n in range(8):
        block = jnp.concatenate([nw[mi[n, s]] for s in range(16)], axis=0)
        nfar[n * 32:(n + 1) * 32, :] = dot(zn[n * 32:(n + 1) * 32, :], block, 1, 0)

    def leaves(t, carry):
        for u in range(4):
            n = t * 4 + u
            block = jnp.concatenate([cw[li[s, n]] for s in range(16)], axis=0)
            rows = pl.ds(pl.multiple_of(n * 32, 32), 32)
            far[rows, :] = dot(zl[rows, :], block, 1, 0)
        return carry

    lax.fori_loop(0, 16, leaves, 0)


def table_kernel(y, received, after, own):
    half = y.shape[0]
    own[0:half, :] = y[...]
    own[half:, :] = received[...]


def down_kernel(dl, gl, own, other, zd, zg, dt, nt, tl, b, far, nfar, near, out, nds):
    cp = lax.axis_index("coarse")

    def pick(coarse, row, count):
        at = (coarse ^ cp) >> 1
        rows = pl.ds(pl.multiple_of(at * TAB + row, 16), count)
        same = ((coarse ^ cp) & 1) == 0
        return jnp.where(same, own[rows, :].astype(F32), other[rows, :].astype(F32))

    parts = []
    for s in range(8):
        x = pick(gl[0, s], 128, 16)
        parts += [x.astype(BF), pltpu.roll(x, 64, 1).astype(BF)]
    gf = dot(zg[...], jnp.concatenate(parts, axis=0), 1, 0).astype(BF)
    parts = []
    for s in range(16):
        d = dl[0, s]
        x = pick(d >> 3, ((d & 7) >> 1) * 32, 32)
        parts.append(jnp.where((d & 1) == 1, pltpu.roll(x, 64, 1), x).astype(BF))
    df = dot(zd[...], jnp.concatenate(parts, axis=0), 1, 0) + dot(dt[...], gf, 1, 0)
    nds[...] = dot(nt[...], df.astype(BF), 1, 0)
    mask = diagonal_mask()
    for n in range(8):
        nf = (nds[pl.ds(n, 32, stride=8), :] + nfar[n * 32:(n + 1) * 32, :]).astype(BF)
        rows = slice(n * 256, (n + 1) * 256)
        lf = (dot(tl[rows, :32], nf, 1, 0) + far[rows, :]).astype(BF)
        for h in range(2):
            g = 2 * n + h
            lanes = slice(g * 256, (g + 1) * 256)
            bg = b[:, lanes]
            bd = jnp.concatenate([bg, bg, bg, bg], axis=0) * mask
            x = dot(lf[h * 128:(h + 1) * 128, :64], bd, 0, 0)
            out[:, lanes] = (x + near[:, lanes]).astype(BF)


AN = pl.BlockSpec(memory_space=pl.ANY)
HB = pl.BlockSpec(memory_space=pltpu.HBM)
VM = pl.BlockSpec(memory_space=pltpu.VMEM)
SM = pl.BlockSpec(memory_space=pltpu.SMEM)


def shape(dims, dtype=BF):
    return jax.ShapeDtypeStruct(dims, dtype)


def params(mib):
    return pltpu.CompilerParams(vmem_limit_bytes=mib * MB)


def cost(flops, size):
    return pl.CostEstimate(flops=flops, bytes_accessed=size, transcendentals=0)


def body(
    vectors, leaf_basis, near_blocks, near_index, leaf_transfer, node_transfer, device_transfer,
    leaf_lists, leaf_coupling, node_lists, node_coupling, device_lists, device_coupling,
    group_lists, group_coupling,
):
    nt = jnp.transpose(node_transfer, (0, 2, 1)).reshape(256, 32)
    dt = device_transfer.reshape(32, 32)
    pay, cown, nown, up, dn, tl, fup, fdn = pl.pallas_call(
        up_kernel,
        out_shape=[
            shape((8, 32, 128)), shape((1024, 128)), shape((128, 128)),
            shape((ROWS1, 128)), shape((ROWS1, 128)), shape((2048, 128)),
            shape((512, 128)), shape((512, 128)),
        ],
        in_specs=[HB] * 5,
        out_specs=[VM] * 8,
        scratch_shapes=[
            pltpu.VMEM((2048, 64), BF), pltpu.VMEM((2048, 128), F32), pltpu.VMEM((256, 128), F32),
            pltpu.VMEM((32, 32, 64), BF), pltpu.VMEM((64, 4096), BF), pltpu.VMEM((32, 4096), BF),
            pltpu.VMEM((256, 32), BF), pltpu.VMEM((32, 32), BF), pltpu.SemaphoreType.DMA((5,)),
        ],
        compiler_params=params(58),
        cost_estimate=cost(10**9, 4 * 10**6),
        name="up_pass",
    )(vectors, leaf_basis, leaf_transfer, nt, dt)

    coarse, leafs = lax.axis_size("coarse"), lax.axis_size("leaf")
    r = lax.all_to_all(pay, "leaf", 0, 0, tiled=True)

    def shift(x, axis, step):
        size = lax.axis_size(axis)
        pairs = [(i, i + step) for i in range(size) if 0 <= i + step < size]
        return lax.ppermute(x, axis, pairs)

    bef, aft = shift(up, "coarse", 1), shift(dn, "coarse", -1)

    zl, zn, zd, zg, near_ix, leaf_ix, node_ix = pl.pallas_call(
        prep_kernel,
        out_shape=[
            shape((2048, 512)), shape((256, 512)), shape((32, 512)), shape((32, 256)),
            shape((12, 64), jnp.int32), shape((16, 64), jnp.int32), shape((8, 16), jnp.int32),
        ],
        in_specs=[VM] * 3 + [HB] * 4,
        out_specs=[VM] * 7,
        scratch_shapes=[
            pltpu.VMEM((4, 2048, 128), F32), pltpu.VMEM((256, 128), F32),
            pltpu.VMEM((16, 32, 32, 64), BF), pltpu.VMEM((16, 32, 8, 32), BF),
            pltpu.VMEM((16, 32, 32), BF), pltpu.VMEM((8, 32, 32), BF),
            pltpu.SemaphoreType.DMA((7,)),
        ],
        compiler_params=params(48),
        cost_estimate=cost(10**9, 8 * 10**6),
        name="coupling_layout",
    )(
        near_index, leaf_lists, node_lists.T, leaf_coupling, jnp.transpose(node_coupling, (0, 1, 3, 2)),
        device_coupling.reshape(16, 32, 32), group_coupling.reshape(8, 32, 32),
    )

    up2, dn2 = pl.pallas_call(
        pack_kernel,
        out_shape=[shape((ROWS2, 128))] * 2,
        in_specs=[HB] * 6,
        out_specs=[VM] * 2,
        scratch_shapes=[pltpu.SemaphoreType.DMA((24,))],
        compiler_params=params(58),
        cost_estimate=cost(1000, 10**6),
        name="halo_pack",
    )(fup, fdn, cown, nown, bef, aft)
    lb, la = shift(up2, "leaf", 1), shift(dn2, "leaf", -1)

    y = pl.pallas_call(
        group_kernel,
        out_shape=shape((TAB, 128)),
        in_specs=[VM, HB],
        out_specs=VM,
        compiler_params=params(8),
        cost_estimate=cost(1000, 10**5),
        name="group_sum",
    )(r, up2)
    flip = lambda x, bit: lax.ppermute(x, "coarse", [(i, i ^ bit) for i in range(coarse)])
    for bit in (2, 4, 8):
        y = jnp.concatenate([y, flip(y, bit)], axis=0)
    received = flip(y, 16)

    near = pl.pallas_call(
        near_kernel,
        out_shape=shape((64, 4096), F32),
        in_specs=[AN, VM, VM, VM, VM, VM, HB],
        out_specs=VM,
        scratch_shapes=[
            pltpu.VMEM((144, 64, 128), BF), pltpu.VMEM((144, 64, 128), BF),
            pltpu.VMEM((4, 128, 768), BF), pltpu.SMEM((12, 64), jnp.int32),
            pltpu.VMEM((8, 768, 512), BF), pltpu.SemaphoreType.DMA((9,)),
        ],
        compiler_params=params(48),
        cost_estimate=cost(4 * 10**9, 16 * 10**6),
        name="near_field",
    )(near_ix, vectors, bef, aft, lb, la, near_blocks.reshape(768, 4096))

    own = pl.pallas_call(
        table_kernel,
        out_shape=shape((16 * TAB, 128)),
        in_specs=[VM, VM, AN],
        out_specs=VM,
        compiler_params=params(8),
        cost_estimate=cost(1000, 10**6),
        name="table_join",
    )(y, received, near)
    other = flip(own, 1)

    far, nfar = pl.pallas_call(
        far_kernel,
        out_shape=[shape((2048, 128), F32), shape((256, 128), F32)],
        in_specs=[AN] * 2 + [VM] * 8,
        out_specs=[VM] * 2,
        scratch_shapes=[
            pltpu.VMEM((256, 32, 128), BF), pltpu.VMEM((72, 32, 128), BF),
            pltpu.SMEM((16, 64), jnp.int32), pltpu.SMEM((8, 16), jnp.int32),
            pltpu.SemaphoreType.DMA((2,)),
        ],
        compiler_params=params(32),
        cost_estimate=cost(4 * 10**9, 16 * 10**6),
        name="far_field",
    )(leaf_ix, node_ix, cown, nown, bef, aft, lb, la, zl, zn)

    return pl.pallas_call(
        down_kernel,
        out_shape=shape((64, 4096)),
        in_specs=[SM] * 2 + [VM] * 11,
        out_specs=VM,
        scratch_shapes=[pltpu.VMEM((256, 128), F32)],
        compiler_params=params(32),
        cost_estimate=cost(10**9, 4 * 10**6),
        name="down_pass",
    )(
        device_lists.reshape(1, 16), group_lists.reshape(1, 8), own, other, zd, zg, dt, nt, tl,
        leaf_basis, far, nfar, near,
    )


def solution(mesh):
    both = ("coarse", "leaf")
    placed = (
        P(None, both), P(None, both), P(None, None, both), P(None, both), P(None, None, both),
        P(None, None, both), P(None, None, both), P(None, both), P(None, None, None, both),
        P(None, both), P(None, None, None, both), P(None, both), P(None, None, None, both),
        P(None, "coarse"), P(None, None, None, "coarse"),
    )
    return jax.shard_map(
        body, mesh=mesh, in_specs=placed, out_specs=P(None, both), check_vma=False
    )
```

```python
import jax
import jax.numpy as jnp
from jax import lax
from jax.experimental import pallas as pl
from jax.experimental.pallas import tpu as pltpu
from jax.sharding import PartitionSpec as P

BF = jnp.bfloat16
F32 = jnp.float32
V1, C1, N1 = 512, 512, 128
V2, C2, N2 = 768, 1024, 384
ROWS1 = V1 + C1 + N1
ROWS2 = V2 + C2 + N2
TAB = 144
MB = 1024 * 1024


def dot(a, b, ca, cb):
    return lax.dot_general(a, b, (((ca,), (cb,)), ((), ())), preferred_element_type=F32)


def copies(pairs, sems):
    started = [pltpu.make_async_copy(src, dst, sems.at[i]) for i, (src, dst) in enumerate(pairs)]
    for c in started:
        c.start()
    return started


def eye(n):
    rows = lax.broadcasted_iota(jnp.int32, (n, n), 0)
    cols = lax.broadcasted_iota(jnp.int32, (n, n), 1)
    return jnp.where(rows == cols, 1.0, 0.0).astype(BF)


def diagonal_mask():
    rows = lax.broadcasted_iota(jnp.int32, (128, 256), 0)
    cols = lax.broadcasted_iota(jnp.int32, (128, 256), 1)
    return jnp.where((rows >> 5) == (cols >> 6), 1.0, 0.0).astype(BF)


def low_lanes(rows):
    return lax.broadcasted_iota(jnp.int32, (rows, 128), 1) < 64


def node_parts(node):
    block, rest = node >> 3, node & 7
    return 2 * (block >> 3) + (rest >> 2), 2 * (block & 7) + ((rest >> 1) & 1), rest & 1


def up_kernel(
    v_hbm, b_hbm, lt_hbm, nt_hbm, dt_hbm, near_hbm, leaf_hbm, node_hbm,
    pay, cown, nown, ma, mb, tl, faces, near_ix, leaf_ix, node_ix,
    ct, tls, ncs, lt, v, b, nt, dt, near_in, leaf_in, node_in, sems,
):
    loads = copies(
        [
            (lt_hbm, lt), (v_hbm, v), (b_hbm, b), (nt_hbm, nt), (dt_hbm, dt),
            (near_hbm, near_in), (leaf_hbm, leaf_in), (node_hbm, node_in),
        ],
        sems,
    )
    ident = eye(64)
    loads[0].wait()
    for k in range(32):
        tls[pl.ds(k, 64, stride=32), :] = dot(
            ident, jnp.concatenate([lt[k], jnp.zeros((96, 64), BF)], axis=0), 1, 1
        )
    tl[...] = tls[...].astype(BF)
    for c in loads[1:]:
        c.wait()
    cp, lp = lax.axis_index("coarse"), lax.axis_index("leaf")
    num = near_in[...]
    px, py, pz = node_parts(num >> 3)
    lx = 2 * px + ((num >> 2) & 1) - 4 * cp + 1
    ly = 2 * py + ((num >> 1) & 1) - 4 * lp + 1
    near_ix[...] = jnp.clip((lx * 6 + ly) * 4 + 2 * pz + (num & 1), 0, 143)
    num = leaf_in[...]
    px, py, pz = node_parts(num >> 3)
    at = ((px - 2 * cp + 1) * 4 + (py - 2 * lp + 1)) * 2 + pz
    leaf_ix[...] = jnp.clip(at * 8 + (num & 7), 0, 255)
    px, py, pz = node_parts(node_in[...])
    at = ((px - 2 * cp + 2) * 6 + (py - 2 * lp + 2)) * 2 + pz
    node_ix[...] = jnp.clip(at, 0, 71)
    mask = diagonal_mask()
    for g in range(16):
        lanes = slice(g * 256, (g + 1) * 256)
        bg = b[:, lanes]
        bd = jnp.concatenate([bg, bg, bg, bg], axis=0) * mask
        c = dot(bd, v[:, lanes], 1, 1)
        ct[g * 128:(g + 1) * 128, :] = c.astype(BF)
        for h in range(2):
            pair = jnp.concatenate([c[h * 64:h * 64 + 32], c[h * 64 + 32:h * 64 + 64]], axis=1)
            cown[(2 * g + h) * 32:(2 * g + h + 1) * 32, :] = pair.astype(BF)
    for m in range(4):
        parts = []
        for n in (2 * m, 2 * m + 1):
            rows = slice(n * 256, (n + 1) * 256)
            nc = dot(tl[rows, :32], ct[rows, :], 0, 0)
            parts.append(nc)
            wide = jnp.concatenate([nc, nc], axis=1)
            ncs[pl.ds(n, 32, stride=8), :] = wide.astype(BF).astype(F32)
        nown[m * 32:(m + 1) * 32, :] = jnp.concatenate(parts, axis=1).astype(BF)
    dc = dot(nt[...], ncs[...].astype(BF), 0, 0)
    terms = dot(dt[...], dc.astype(BF), 0, 0)
    message = jnp.where(low_lanes(32), dc, terms).astype(BF)
    for z in range(8):
        pay[z] = message
    for out, side in ((ma, 1 - (cp & 1)), (mb, cp & 1)):
        for j in range(2):
            for k in range(2):
                for bb in range(2):
                    at = ((2 * j + k) * 2 + bb) * 64
                    first = ((2 * j + k) * 8 + 2 * bb) * 64 + side * 2304
                    out[at:at + 64, :] = v[:, pl.ds(pl.multiple_of(first, 128), 128)]
        out[V1:V1 + C1, :] = cown[pl.ds(pl.multiple_of(side * 512, 512), 512), :]
        out[V1 + C1:, :] = nown[...]
    for j in range(2):
        for i in range(2):
            for a in range(2):
                for k in range(2):
                    at = j * 512 + ((i * 2 + a) * 2 + k) * 64
                    first = ((i * 4 + k) * 8 + 4 * a + 18 * j) * 64
                    faces[at:at + 64, :] = v[:, first:first + 128]


def pack_kernel(faces, cown, nown, ra, rb, qa, qb):
    lp = lax.axis_index("leaf")
    for out, j in ((qa, 1 - (lp & 1)), (qb, lp & 1)):
        rows = [(faces, j * 512, 512)]
        for side in (ra, rb):
            rows += [(side, (5 * j + 2 * k) * 64, 64) for k in range(2)]
        rows += [(cown, (i * 2 + j) * 256, 256) for i in range(2)]
        rows += [(side, V1 + j * 256, 256) for side in (ra, rb)]
        rows += [(nown, 0, 128), (ra, V1 + C1, 128), (rb, V1 + C1, 128)]
        at = 0
        for side, first, count in rows:
            if not isinstance(first, int):
                first = pl.multiple_of(first, 64)
            out[at:at + count, :] = side[pl.ds(first, count), :]
            at += count


def group_kernel(r, after, y):
    low = low_lanes(32)
    total = jnp.zeros((32, 128), F32)
    for m in range(4):
        lo, hi = r[2 * m].astype(F32), r[2 * m + 1].astype(F32)
        total = total + lo + hi
        y[m * 32:(m + 1) * 32, :] = jnp.where(low, lo, pltpu.roll(hi, 64, 1)).astype(BF)
    swapped = pltpu.roll(total, 64, 1)
    y[128:144, :] = jnp.where(low_lanes(16), swapped[0:16], total[16:32]).astype(BF)


def transpose_half(base, s_hbm, zl, zs, s, sems):
    loads = copies(
        [
            (s_hbm.at[pl.ds(base, 8), pl.ds(8 * q, 8)], s.at[:, pl.ds(8 * q, 8)])
            for q in range(4)
        ],
        sems,
    )
    ident = eye(64)
    for j in range(32):
        if j % 8 == 0:
            loads[j // 8].wait()
        x = s[:, j].reshape(256, 64)
        t = dot(ident, x, 1, 1) if j % 2 else x.T.astype(F32)
        for q in range(2):
            zs[q, pl.ds(j, 64, stride=32), :] = t[:, q * 128:(q + 1) * 128]
    for q in range(2):
        zl[:, q * 128:(q + 1) * 128] = zs[q].astype(BF)


def first_layout_kernel(s_hbm, zl, zs, s, sems):
    transpose_half(0, s_hbm, zl, zs, s, sems)


def second_layout_kernel(
    s_hbm, sn_hbm, sd_hbm, sg_hbm, zl, zn, zd, zg, zs, s, ns, sn, sd, sg, sems, more
):
    loads = copies([(sn_hbm, sn), (sd_hbm, sd), (sg_hbm, sg)], more)
    transpose_half(8, s_hbm, zl, zs, s, sems)
    for c in loads:
        c.wait()
    for q in range(4):
        parts = [sn[4 * q + i].astype(F32).reshape(256, 32) for i in range(4)]
        ns[...] = jnp.concatenate(parts, axis=1)
        for n in range(8):
            zn[n * 32:(n + 1) * 32, q * 128:(q + 1) * 128] = ns[pl.ds(n, 32, stride=8), :].astype(BF)
        parts = [sd[4 * q + i].astype(F32) for i in range(4)]
        zd[:, q * 128:(q + 1) * 128] = jnp.concatenate(parts, axis=1).astype(BF)
    for q in range(2):
        parts = [sg[4 * q + i].astype(F32) for i in range(4)]
        zg[:, q * 128:(q + 1) * 128] = jnp.concatenate(parts, axis=1).astype(BF)


def near_kernel(ix_any, v, ra, rb, qa, qb, blocks_hbm, out, low, high, picked, ix, blocks, sems):
    loads = copies(
        [(ix_any, ix)]
        + [(blocks_hbm.at[:, pl.ds(512 * t, 512)], blocks.at[t]) for t in range(8)],
        sems,
    )
    mask = low_lanes(64)
    odd_c, odd_l = lax.axis_index("coarse") & 1, lax.axis_index("leaf") & 1

    def table():
        def put(wx, wy, k, x):
            at = (wx * 6 + wy) * 4 + 2 * k
            x = x.astype(F32)
            swapped = pltpu.roll(x, 64, 1)
            low[at] = jnp.where(mask, x, 0.0).astype(BF)
            high[at] = jnp.where(mask, 0.0, swapped).astype(BF)
            low[at + 1] = jnp.where(mask, swapped, 0.0).astype(BF)
            high[at + 1] = jnp.where(mask, 0.0, x).astype(BF)

        for i in range(2):
            for j in range(2):
                for k in range(2):
                    for a in range(2):
                        for bb in range(2):
                            first = (((i * 2 + j) * 2 + k) * 8 + 4 * a + 2 * bb) * 64
                            put(1 + 2 * i + a, 1 + 2 * j + bb, k, v[:, first:first + 128])
        for side, wx in ((ra, 5 - 5 * odd_c), (rb, 5 * odd_c)):
            for j in range(2):
                for k in range(2):
                    for bb in range(2):
                        first = ((2 * j + k) * 2 + bb) * 64
                        put(wx, 1 + 2 * j + bb, k, side[first:first + 64, :])
        for side, wy in ((qa, 5 - 5 * odd_l), (qb, 5 * odd_l)):
            for i in range(2):
                for a in range(2):
                    for k in range(2):
                        first = ((i * 2 + a) * 2 + k) * 64
                        put(1 + 2 * i + a, wy, k, side[first:first + 64, :])
            for wx, base in ((5 - 5 * odd_c, 8), (5 * odd_c, 10)):
                for k in range(2):
                    first = (base + k) * 64
                    put(wx, wy, k, side[first:first + 64, :])

    table()
    loads[0].wait()

    def chunk(t, carry):
        pltpu.make_async_copy(
            blocks_hbm.at[:, pl.ds(pl.multiple_of(512 * t, 512), 512)], blocks.at[t], sems.at[t + 1]
        ).wait()
        for q in range(4):
            for i in range(2):
                leaf = t * 8 + 2 * q + i
                for sp in range(6):
                    picked[q, i * 64:(i + 1) * 64, sp * 128:(sp + 1) * 128] = (
                        low[ix[2 * sp, leaf]] + high[ix[2 * sp + 1, leaf]]
                    )
            r = dot(picked[q], blocks[t, :, q * 128:(q + 1) * 128], 1, 0)
            lanes = pl.ds(pl.multiple_of(t * 512 + q * 128, 128), 128)
            out[:, lanes] = jnp.where(mask, r[:64], r[64:])
        return carry

    lax.fori_loop(0, 8, chunk, 0)


def far_kernel(
    li_any, mi_any, cown, nown, ra, rb, qa, qb, za, zb, zn, far, nfar, low, high, nw, li, mi, sems
):
    loads = copies([(li_any, li), (mi_any, mi)], sems)
    mask = low_lanes(32)

    def put_leaves(nwx, nwy, k, side, first):
        for p in range(4):
            x = side[first + p * 32:first + (p + 1) * 32, :].astype(F32)
            at = ((nwx * 4 + nwy) * 2 + k) * 8 + 2 * p
            swapped = pltpu.roll(x, 64, 1)
            low[at] = jnp.where(mask, x, 0.0).astype(BF)
            high[at] = jnp.where(mask, 0.0, swapped).astype(BF)
            low[at + 1] = jnp.where(mask, swapped, 0.0).astype(BF)
            high[at + 1] = jnp.where(mask, 0.0, x).astype(BF)

    def put_nodes(nwx, nwy, side, first):
        x = side[first:first + 32, :]
        at = (nwx * 6 + nwy) * 2
        nw[at] = x
        nw[at + 1] = pltpu.roll(x.astype(F32), 64, 1).astype(BF)

    odd_c, odd_l = lax.axis_index("coarse") & 1, lax.axis_index("leaf") & 1
    in_x, in_y = ((ra, 1 - odd_c), (rb, odd_c)), ((qa, 1 - odd_l), (qb, odd_l))
    for i in range(2):
        for j in range(2):
            put_nodes(2 + i, 2 + j, nown, (i * 2 + j) * 32)
            for side, after in in_x:
                put_nodes(4 * after + i, 2 + j, side, V1 + C1 + (i * 2 + j) * 32)
            for side, after in in_y:
                first = V2 + C2 + (i * 2 + j) * 32
                put_nodes(2 + i, 4 * after + j, side, first)
                put_nodes(4 - 4 * odd_c + i, 4 * after + j, side, first + 128)
                put_nodes(4 * odd_c + i, 4 * after + j, side, first + 256)
            for k in range(2):
                put_leaves(1 + i, 1 + j, k, cown, ((i * 2 + j) * 2 + k) * 128)
    for j in range(2):
        for k in range(2):
            for side, after in in_x:
                put_leaves(3 * after, 1 + j, k, side, V1 + (2 * j + k) * 128)
    for side, after in in_y:
        for k in range(2):
            for i in range(2):
                put_leaves(1 + i, 3 * after, k, side, V2 + (2 * i + k) * 128)
            put_leaves(3 - 3 * odd_c, 3 * after, k, side, V2 + 512 + k * 128)
            put_leaves(3 * odd_c, 3 * after, k, side, V2 + 768 + k * 128)

    for c in loads:
        c.wait()
    for n in range(8):
        block = jnp.concatenate([nw[mi[n, s]] for s in range(16)], axis=0)
        nfar[n * 32:(n + 1) * 32, :] = dot(zn[n * 32:(n + 1) * 32, :], block, 1, 0)

    def leaves(t, carry):
        for u in range(4):
            n = t * 8 + 2 * u
            block = jnp.concatenate(
                [low[li[s, n]] + high[li[s, n + 1]] for s in range(16)], axis=0
            )
            rows = pl.ds(pl.multiple_of(n * 32, 64), 64)
            r = dot(za[rows, :], block[:256], 1, 0) + dot(zb[rows, :], block[256:], 1, 0)
            far[pl.ds(pl.multiple_of(n * 32, 32), 32), :] = r[:32]
            far[pl.ds(pl.multiple_of(n * 32 + 32, 32), 32), :] = pltpu.roll(r[32:], 64, 1)
        return carry

    lax.fori_loop(0, 8, leaves, 0)


def table_kernel(y, received, after, own):
    half = y.shape[0]
    own[0:half, :] = y[...]
    own[half:, :] = received[...]


def down_kernel(dl, gl, own, other, zd, zg, dt, nt, tl, b, far, nfar, near, out, nds):
    cp = lax.axis_index("coarse")

    def pick(coarse, row, count):
        at = (coarse ^ cp) >> 1
        rows = pl.ds(pl.multiple_of(at * TAB + row, 16), count)
        same = ((coarse ^ cp) & 1) == 0
        return jnp.where(same, own[rows, :].astype(F32), other[rows, :].astype(F32))

    parts = []
    for s in range(8):
        x = pick(gl[0, s], 128, 16)
        parts += [x.astype(BF), pltpu.roll(x, 64, 1).astype(BF)]
    gf = dot(zg[...], jnp.concatenate(parts, axis=0), 1, 0).astype(BF)
    parts = []
    for s in range(16):
        d = dl[0, s]
        x = pick(d >> 3, ((d & 7) >> 1) * 32, 32)
        parts.append(jnp.where((d & 1) == 1, pltpu.roll(x, 64, 1), x).astype(BF))
    df = dot(zd[...], jnp.concatenate(parts, axis=0), 1, 0) + dot(dt[...], gf, 1, 0)
    nds[...] = dot(nt[...], df.astype(BF), 1, 0)
    mask = diagonal_mask()
    for n in range(8):
        nf = (nds[pl.ds(n, 32, stride=8), :] + nfar[n * 32:(n + 1) * 32, :]).astype(BF)
        rows = slice(n * 256, (n + 1) * 256)
        lf = (dot(tl[rows, :32], nf, 1, 0) + far[rows, :]).astype(BF)
        for h in range(2):
            g = 2 * n + h
            lanes = slice(g * 256, (g + 1) * 256)
            bg = b[:, lanes]
            bd = jnp.concatenate([bg, bg, bg, bg], axis=0) * mask
            x = dot(lf[h * 128:(h + 1) * 128, :64], bd, 0, 0)
            out[:, lanes] = (x + near[:, lanes]).astype(BF)


AN = pl.BlockSpec(memory_space=pl.ANY)
HB = pl.BlockSpec(memory_space=pltpu.HBM)
VM = pl.BlockSpec(memory_space=pltpu.VMEM)
SM = pl.BlockSpec(memory_space=pltpu.SMEM)


def shape(dims, dtype=BF):
    return jax.ShapeDtypeStruct(dims, dtype)


def params(mib):
    return pltpu.CompilerParams(vmem_limit_bytes=mib * MB)


def cost(flops, size):
    return pl.CostEstimate(flops=flops, bytes_accessed=size, transcendentals=0)


def body(
    vectors, leaf_basis, near_blocks, near_index, leaf_transfer, node_transfer, device_transfer,
    leaf_lists, leaf_coupling, node_lists, node_coupling, device_lists, device_coupling,
    group_lists, group_coupling,
):
    nt = jnp.transpose(node_transfer, (0, 2, 1)).reshape(256, 32)
    dt = device_transfer.reshape(32, 32)
    pay, cown, nown, ma, mb, tl, faces, near_ix, leaf_ix, node_ix = pl.pallas_call(
        up_kernel,
        out_shape=[
            shape((8, 32, 128)), shape((1024, 128)), shape((128, 128)),
            shape((ROWS1, 128)), shape((ROWS1, 128)), shape((2048, 128)),
            shape((1024, 128)),
            shape((12, 64), jnp.int32), shape((16, 64), jnp.int32), shape((8, 16), jnp.int32),
        ],
        in_specs=[HB] * 8,
        out_specs=[VM] * 10,
        scratch_shapes=[
            pltpu.VMEM((2048, 64), BF), pltpu.VMEM((2048, 128), F32), pltpu.VMEM((256, 128), F32),
            pltpu.VMEM((32, 32, 64), BF), pltpu.VMEM((64, 4096), BF), pltpu.VMEM((32, 4096), BF),
            pltpu.VMEM((256, 32), BF), pltpu.VMEM((32, 32), BF), pltpu.VMEM((12, 64), jnp.int32),
            pltpu.VMEM((16, 64), jnp.int32), pltpu.VMEM((8, 16), jnp.int32),
            pltpu.SemaphoreType.DMA((8,)),
        ],
        compiler_params=params(58),
        cost_estimate=cost(10**6, 10**5),
        name="up_pass",
    )(vectors, leaf_basis, leaf_transfer, nt, dt, near_index, leaf_lists, node_lists.T)

    coarse, leafs = lax.axis_size("coarse"), lax.axis_size("leaf")
    r = lax.all_to_all(pay, "leaf", 0, 0, tiled=True)

    def swap(x, axis, first):
        size = lax.axis_size(axis)
        pairs = [(i, i + 1) for i in range(first, size - 1, 2)]
        return lax.ppermute(x, axis, pairs + [(j, i) for i, j in pairs])

    ra, rb = swap(ma, "coarse", 0), swap(mb, "coarse", 1)

    half = [pltpu.VMEM((2, 2048, 128), F32), pltpu.VMEM((8, 32, 32, 64), BF)]
    za = pl.pallas_call(
        first_layout_kernel,
        out_shape=shape((2048, 256)),
        in_specs=[HB],
        out_specs=VM,
        scratch_shapes=half + [pltpu.SemaphoreType.DMA((4,))],
        compiler_params=params(50),
        cost_estimate=cost(1000, 1000000),
        name="first_layout",
    )(leaf_coupling)
    zb, zn, zd, zg = pl.pallas_call(
        second_layout_kernel,
        out_shape=[shape((2048, 256)), shape((256, 512)), shape((32, 512)), shape((32, 256))],
        in_specs=[HB] * 4,
        out_specs=[VM] * 4,
        scratch_shapes=half + [
            pltpu.VMEM((256, 128), F32), pltpu.VMEM((16, 32, 8, 32), BF),
            pltpu.VMEM((16, 32, 32), BF), pltpu.VMEM((8, 32, 32), BF),
            pltpu.SemaphoreType.DMA((4,)), pltpu.SemaphoreType.DMA((3,)),
        ],
        compiler_params=params(50),
        cost_estimate=cost(1000, 1000000),
        name="second_layout",
    )(
        leaf_coupling, jnp.transpose(node_coupling, (0, 1, 3, 2)),
        device_coupling.reshape(16, 32, 32), group_coupling.reshape(8, 32, 32),
    )

    sa, sb = pl.pallas_call(
        pack_kernel,
        out_shape=[shape((ROWS2, 128))] * 2,
        in_specs=[VM] * 5,
        out_specs=[VM] * 2,
        compiler_params=params(8),
        cost_estimate=cost(1000, 10000000),
        name="halo_pack",
    )(faces, cown, nown, ra, rb)
    qa, qb = swap(sa, "leaf", 0), swap(sb, "leaf", 1)

    y = pl.pallas_call(
        group_kernel,
        out_shape=shape((TAB, 128)),
        in_specs=[VM, AN],
        out_specs=VM,
        compiler_params=params(8),
        cost_estimate=cost(1000, 10**5),
        name="group_sum",
    )(r, za)
    flip = lambda x, bit: lax.ppermute(x, "coarse", [(i, i ^ bit) for i in range(coarse)])

    def join(first, second, after):
        return pl.pallas_call(
            table_kernel,
            out_shape=shape((2 * first.shape[0], 128)),
            in_specs=[VM, VM, AN],
            out_specs=VM,
            compiler_params=params(8),
            cost_estimate=cost(1000, 10**5),
            name="table_join",
        )(first, second, after)


    y = join(y, flip(y, 2), sa)
    y = jnp.concatenate([y, flip(y, 4)], axis=0)
    received = flip(y, 8)

    near = pl.pallas_call(
        near_kernel,
        out_shape=shape((64, 4096), F32),
        in_specs=[AN, VM, VM, VM, VM, VM, HB],
        out_specs=VM,
        scratch_shapes=[
            pltpu.VMEM((144, 64, 128), BF), pltpu.VMEM((144, 64, 128), BF),
            pltpu.VMEM((4, 128, 768), BF), pltpu.SMEM((12, 64), jnp.int32),
            pltpu.VMEM((8, 768, 512), BF), pltpu.SemaphoreType.DMA((9,)),
        ],
        compiler_params=params(48),
        cost_estimate=cost(1000, 1000000),
        name="near_field",
    )(near_ix, vectors, ra, rb, qa, qb, near_blocks.reshape(768, 4096))


    y = join(y, received, zn)
    received = flip(y, 16)

    far, nfar = pl.pallas_call(
        far_kernel,
        out_shape=[shape((2048, 128), F32), shape((256, 128), F32)],
        in_specs=[AN] * 2 + [VM] * 9,
        out_specs=[VM] * 2,
        scratch_shapes=[
            pltpu.VMEM((256, 32, 128), BF), pltpu.VMEM((256, 32, 128), BF),
            pltpu.VMEM((72, 32, 128), BF), pltpu.SMEM((16, 64), jnp.int32), pltpu.SMEM((8, 16), jnp.int32),
            pltpu.SemaphoreType.DMA((2,)),
        ],
        compiler_params=params(32),
        cost_estimate=cost(1000, 1000000),
        name="far_field",
    )(leaf_ix, node_ix, cown, nown, ra, rb, qa, qb, za, zb, zn)

    own = join(y, received, near)
    other = flip(own, 1)

    return pl.pallas_call(
        down_kernel,
        out_shape=shape((64, 4096)),
        in_specs=[SM] * 2 + [VM] * 11,
        out_specs=VM,
        scratch_shapes=[pltpu.VMEM((256, 128), F32)],
        compiler_params=params(32),
        cost_estimate=cost(10**6, 10**5),
        name="down_pass",
    )(
        device_lists.reshape(1, 16), group_lists.reshape(1, 8), own, other, zd, zg, dt, nt, tl,
        leaf_basis, far, nfar, near,
    )


def solution(mesh):
    both = ("coarse", "leaf")
    placed = (
        P(None, both), P(None, both), P(None, None, both), P(None, both), P(None, None, both),
        P(None, None, both), P(None, None, both), P(None, both), P(None, None, None, both),
        P(None, both), P(None, None, None, both), P(None, both), P(None, None, None, both),
        P(None, "coarse"), P(None, None, None, "coarse"),
    )
    return jax.shard_map(
        body, mesh=mesh, in_specs=placed, out_specs=P(None, both), check_vma=False
    )
```

```python
import jax
import jax.numpy as jnp
from jax import lax
from jax.experimental import pallas as pl
from jax.experimental.pallas import tpu as pltpu
from jax.sharding import PartitionSpec as P

BF = jnp.bfloat16
F32 = jnp.float32
V1, C1, N1 = 512, 512, 128
V2, C2, N2 = 768, 1024, 384
ROWS1 = V1 + C1 + N1
ROWS2 = V2 + C2 + N2
TAB = 144
MB = 1024 * 1024


def dot(a, b, ca, cb):
    return lax.dot_general(a, b, (((ca,), (cb,)), ((), ())), preferred_element_type=F32)


def copies(pairs, sems):
    started = [pltpu.make_async_copy(src, dst, sems.at[i]) for i, (src, dst) in enumerate(pairs)]
    for c in started:
        c.start()
    return started


def eye(n):
    rows = lax.broadcasted_iota(jnp.int32, (n, n), 0)
    cols = lax.broadcasted_iota(jnp.int32, (n, n), 1)
    return jnp.where(rows == cols, 1.0, 0.0).astype(BF)


def diagonal_mask():
    rows = lax.broadcasted_iota(jnp.int32, (128, 256), 0)
    cols = lax.broadcasted_iota(jnp.int32, (128, 256), 1)
    return jnp.where((rows >> 5) == (cols >> 6), 1.0, 0.0).astype(BF)


def low_lanes(rows):
    return lax.broadcasted_iota(jnp.int32, (rows, 128), 1) < 64


def node_parts(node):
    block, rest = node >> 3, node & 7
    return 2 * (block >> 3) + (rest >> 2), 2 * (block & 7) + ((rest >> 1) & 1), rest & 1


def up_kernel(
    v_hbm, b_hbm, lt_hbm, nt_hbm, dt_hbm, near_hbm, leaf_hbm, node_hbm,
    pay, cown, nown, ma, mb, tl, faces, near_ix, leaf_ix, node_ix,
    ct, tls, ncs, lt, v, b, nt, dt, near_in, leaf_in, node_in, sems,
):
    loads = copies(
        [
            (lt_hbm, lt), (v_hbm, v), (b_hbm, b), (nt_hbm, nt), (dt_hbm, dt),
            (near_hbm, near_in), (leaf_hbm, leaf_in), (node_hbm, node_in),
        ],
        sems,
    )
    ident = eye(64)
    loads[0].wait()
    for k in range(32):
        tls[pl.ds(k, 64, stride=32), :] = dot(
            ident, jnp.concatenate([lt[k], jnp.zeros((96, 64), BF)], axis=0), 1, 1
        )
    tl[...] = tls[...].astype(BF)
    for c in loads[1:]:
        c.wait()
    cp, lp = lax.axis_index("coarse"), lax.axis_index("leaf")
    num = near_in[...]
    px, py, pz = node_parts(num >> 3)
    lx = 2 * px + ((num >> 2) & 1) - 4 * cp + 1
    ly = 2 * py + ((num >> 1) & 1) - 4 * lp + 1
    near_ix[...] = jnp.clip((lx * 6 + ly) * 4 + 2 * pz + (num & 1), 0, 143)
    num = leaf_in[...]
    px, py, pz = node_parts(num >> 3)
    at = ((px - 2 * cp + 1) * 4 + (py - 2 * lp + 1)) * 2 + pz
    leaf_ix[...] = jnp.clip(at * 8 + (num & 7), 0, 255)
    px, py, pz = node_parts(node_in[...])
    at = ((px - 2 * cp + 2) * 6 + (py - 2 * lp + 2)) * 2 + pz
    node_ix[...] = jnp.clip(at, 0, 71)
    mask = diagonal_mask()
    for g in range(16):
        lanes = slice(g * 256, (g + 1) * 256)
        bg = b[:, lanes]
        bd = jnp.concatenate([bg, bg, bg, bg], axis=0) * mask
        c = dot(bd, v[:, lanes], 1, 1)
        ct[g * 128:(g + 1) * 128, :] = c.astype(BF)
        for h in range(2):
            pair = jnp.concatenate([c[h * 64:h * 64 + 32], c[h * 64 + 32:h * 64 + 64]], axis=1)
            cown[(2 * g + h) * 32:(2 * g + h + 1) * 32, :] = pair.astype(BF)
    for m in range(4):
        parts = []
        for n in (2 * m, 2 * m + 1):
            rows = slice(n * 256, (n + 1) * 256)
            nc = dot(tl[rows, :32], ct[rows, :], 0, 0)
            parts.append(nc)
            wide = jnp.concatenate([nc, nc], axis=1)
            ncs[pl.ds(n, 32, stride=8), :] = wide.astype(BF).astype(F32)
        nown[m * 32:(m + 1) * 32, :] = jnp.concatenate(parts, axis=1).astype(BF)
    dc = dot(nt[...], ncs[...].astype(BF), 0, 0)
    terms = dot(dt[...], dc.astype(BF), 0, 0)
    message = jnp.where(low_lanes(32), dc, terms).astype(BF)
    for z in range(8):
        pay[z] = message
    for out, side in ((ma, 1 - (cp & 1)), (mb, cp & 1)):
        for j in range(2):
            for k in range(2):
                for bb in range(2):
                    at = ((2 * j + k) * 2 + bb) * 64
                    first = ((2 * j + k) * 8 + 2 * bb) * 64 + side * 2304
                    out[at:at + 64, :] = v[:, pl.ds(pl.multiple_of(first, 128), 128)]
        out[V1:V1 + C1, :] = cown[pl.ds(pl.multiple_of(side * 512, 512), 512), :]
        out[V1 + C1:, :] = nown[...]
    for j in range(2):
        for i in range(2):
            for a in range(2):
                for k in range(2):
                    at = j * 512 + ((i * 2 + a) * 2 + k) * 64
                    first = ((i * 4 + k) * 8 + 4 * a + 18 * j) * 64
                    faces[at:at + 64, :] = v[:, first:first + 128]


def pack_kernel(faces, cown, nown, ra, rb, qa, qb):
    lp = lax.axis_index("leaf")
    for out, j in ((qa, 1 - (lp & 1)), (qb, lp & 1)):
        rows = [(faces, j * 512, 512)]
        for side in (ra, rb):
            rows += [(side, (5 * j + 2 * k) * 64, 64) for k in range(2)]
        rows += [(cown, (i * 2 + j) * 256, 256) for i in range(2)]
        rows += [(side, V1 + j * 256, 256) for side in (ra, rb)]
        rows += [(nown, 0, 128), (ra, V1 + C1, 128), (rb, V1 + C1, 128)]
        at = 0
        for side, first, count in rows:
            if not isinstance(first, int):
                first = pl.multiple_of(first, 64)
            out[at:at + count, :] = side[pl.ds(first, count), :]
            at += count


def group_kernel(r, after, y):
    low = low_lanes(32)
    total = jnp.zeros((32, 128), F32)
    for m in range(4):
        lo, hi = r[2 * m].astype(F32), r[2 * m + 1].astype(F32)
        total = total + lo + hi
        y[m * 32:(m + 1) * 32, :] = jnp.where(low, lo, pltpu.roll(hi, 64, 1)).astype(BF)
    swapped = pltpu.roll(total, 64, 1)
    y[128:144, :] = jnp.where(low_lanes(16), swapped[0:16], total[16:32]).astype(BF)


def transpose_half(base, s_hbm, zl, zs, s, sems):
    loads = copies(
        [
            (s_hbm.at[pl.ds(base, 8), pl.ds(8 * q, 8)], s.at[:, pl.ds(8 * q, 8)])
            for q in range(4)
        ],
        sems,
    )
    ident = eye(64)
    for j in range(32):
        if j % 8 == 0:
            loads[j // 8].wait()
        x = s[:, j].reshape(256, 64)
        t = dot(ident, x, 1, 1) if j % 2 else x.T.astype(F32)
        for q in range(2):
            zs[q, pl.ds(j, 64, stride=32), :] = t[:, q * 128:(q + 1) * 128]
    for q in range(2):
        zl[:, q * 128:(q + 1) * 128] = zs[q].astype(BF)


def first_layout_kernel(s_hbm, zl, zs, s, sems):
    transpose_half(0, s_hbm, zl, zs, s, sems)


def second_layout_kernel(
    s_hbm, sn_hbm, sd_hbm, sg_hbm, zl, zn, zd, zg, zs, s, ns, sn, sd, sg, sems, more
):
    loads = copies([(sn_hbm, sn), (sd_hbm, sd), (sg_hbm, sg)], more)
    transpose_half(8, s_hbm, zl, zs, s, sems)
    for c in loads:
        c.wait()
    for q in range(4):
        parts = [sn[4 * q + i].astype(F32).reshape(256, 32) for i in range(4)]
        ns[...] = jnp.concatenate(parts, axis=1)
        for n in range(8):
            zn[n * 32:(n + 1) * 32, q * 128:(q + 1) * 128] = ns[pl.ds(n, 32, stride=8), :].astype(BF)
        parts = [sd[4 * q + i].astype(F32) for i in range(4)]
        zd[:, q * 128:(q + 1) * 128] = jnp.concatenate(parts, axis=1).astype(BF)
    for q in range(2):
        parts = [sg[4 * q + i].astype(F32) for i in range(4)]
        zg[:, q * 128:(q + 1) * 128] = jnp.concatenate(parts, axis=1).astype(BF)


def near_kernel(ix_any, v, ra, rb, qa, qb, blocks_hbm, out, pieces, ix, blocks, sems):
    loads = copies(
        [(ix_any, ix)]
        + [(blocks_hbm.at[:, pl.ds(512 * t, 512)], blocks.at[t]) for t in range(8)],
        sems,
    )
    mask = low_lanes(64)
    odd_c, odd_l = lax.axis_index("coarse") & 1, lax.axis_index("leaf") & 1

    def table():
        def put(wx, wy, k, x):
            at = (wx * 6 + wy) * 4 + 2 * k
            pieces[at] = x
            pieces[at + 1] = pltpu.roll(x.astype(F32), 64, 1).astype(BF)

        for i in range(2):
            for j in range(2):
                for k in range(2):
                    for a in range(2):
                        for bb in range(2):
                            first = (((i * 2 + j) * 2 + k) * 8 + 4 * a + 2 * bb) * 64
                            put(1 + 2 * i + a, 1 + 2 * j + bb, k, v[:, first:first + 128])
        for side, wx in ((ra, 5 - 5 * odd_c), (rb, 5 * odd_c)):
            for j in range(2):
                for k in range(2):
                    for bb in range(2):
                        first = ((2 * j + k) * 2 + bb) * 64
                        put(wx, 1 + 2 * j + bb, k, side[first:first + 64, :])
        for side, wy in ((qa, 5 - 5 * odd_l), (qb, 5 * odd_l)):
            for i in range(2):
                for a in range(2):
                    for k in range(2):
                        first = ((i * 2 + a) * 2 + k) * 64
                        put(1 + 2 * i + a, wy, k, side[first:first + 64, :])
            for wx, base in ((5 - 5 * odd_c, 8), (5 * odd_c, 10)):
                for k in range(2):
                    first = (base + k) * 64
                    put(wx, wy, k, side[first:first + 64, :])

    table()
    loads[0].wait()

    def chunk(t, carry):
        pltpu.make_async_copy(
            blocks_hbm.at[:, pl.ds(pl.multiple_of(512 * t, 512), 512)], blocks.at[t], sems.at[t + 1]
        ).wait()
        for q in range(4):
            lhs = []
            for i in range(2):
                leaf = t * 8 + 2 * q + i
                lhs.append(jnp.concatenate(
                    [
                        jnp.where(mask, pieces[ix[2 * sp, leaf]], pieces[ix[2 * sp + 1, leaf] ^ 1])
                        for sp in range(6)
                    ],
                    axis=1,
                ))
            r = dot(jnp.concatenate(lhs, axis=0), blocks[t, :, q * 128:(q + 1) * 128], 1, 0)
            lanes = pl.ds(pl.multiple_of(t * 512 + q * 128, 128), 128)
            out[:, lanes] = jnp.where(mask, r[:64], r[64:])
        return carry

    lax.fori_loop(0, 8, chunk, 0, unroll=2)


def far_kernel(
    li_any, mi_any, cown, nown, ra, rb, qa, qb, za, zb, zn, far, nfar, pieces, nw, li, mi, sems
):
    loads = copies([(li_any, li), (mi_any, mi)], sems)
    mask = low_lanes(32)

    def put_leaves(nwx, nwy, k, side, first):
        for p in range(4):
            x = side[first + p * 32:first + (p + 1) * 32, :]
            at = ((nwx * 4 + nwy) * 2 + k) * 8 + 2 * p
            pieces[at] = x
            pieces[at + 1] = pltpu.roll(x.astype(F32), 64, 1).astype(BF)

    def put_nodes(nwx, nwy, side, first):
        x = side[first:first + 32, :]
        at = (nwx * 6 + nwy) * 2
        nw[at] = x
        nw[at + 1] = pltpu.roll(x.astype(F32), 64, 1).astype(BF)

    odd_c, odd_l = lax.axis_index("coarse") & 1, lax.axis_index("leaf") & 1
    in_x, in_y = ((ra, 1 - odd_c), (rb, odd_c)), ((qa, 1 - odd_l), (qb, odd_l))
    for i in range(2):
        for j in range(2):
            put_nodes(2 + i, 2 + j, nown, (i * 2 + j) * 32)
            for side, after in in_x:
                put_nodes(4 * after + i, 2 + j, side, V1 + C1 + (i * 2 + j) * 32)
            for side, after in in_y:
                first = V2 + C2 + (i * 2 + j) * 32
                put_nodes(2 + i, 4 * after + j, side, first)
                put_nodes(4 - 4 * odd_c + i, 4 * after + j, side, first + 128)
                put_nodes(4 * odd_c + i, 4 * after + j, side, first + 256)
            for k in range(2):
                put_leaves(1 + i, 1 + j, k, cown, ((i * 2 + j) * 2 + k) * 128)
    for j in range(2):
        for k in range(2):
            for side, after in in_x:
                put_leaves(3 * after, 1 + j, k, side, V1 + (2 * j + k) * 128)
    for side, after in in_y:
        for k in range(2):
            for i in range(2):
                put_leaves(1 + i, 3 * after, k, side, V2 + (2 * i + k) * 128)
            put_leaves(3 - 3 * odd_c, 3 * after, k, side, V2 + 512 + k * 128)
            put_leaves(3 * odd_c, 3 * after, k, side, V2 + 768 + k * 128)

    for c in loads:
        c.wait()
    for n in range(8):
        block = jnp.concatenate([nw[mi[n, s]] for s in range(16)], axis=0)
        nfar[n * 32:(n + 1) * 32, :] = dot(zn[n * 32:(n + 1) * 32, :], block, 1, 0)

    def leaves(t, carry):
        for u in range(4):
            n = t * 8 + 2 * u
            block = jnp.concatenate(
                [jnp.where(mask, pieces[li[s, n]], pieces[li[s, n + 1] ^ 1]) for s in range(16)],
                axis=0,
            )
            rows = pl.ds(pl.multiple_of(n * 32, 64), 64)
            r = dot(za[rows, :], block[:256], 1, 0) + dot(zb[rows, :], block[256:], 1, 0)
            far[pl.ds(pl.multiple_of(n * 32, 32), 32), :] = r[:32]
            far[pl.ds(pl.multiple_of(n * 32 + 32, 32), 32), :] = pltpu.roll(r[32:], 64, 1)
        return carry

    lax.fori_loop(0, 8, leaves, 0, unroll=8)


def table_kernel(y, received, after, own):
    half = y.shape[0]
    own[0:half, :] = y[...]
    own[half:, :] = received[...]


def down_kernel(dl, gl, own, other, zd, zg, dt, nt, tl, b, far, nfar, near, out, nds):
    cp = lax.axis_index("coarse")

    def pick(coarse, row, count):
        at = (coarse ^ cp) >> 1
        rows = pl.ds(pl.multiple_of(at * TAB + row, 16), count)
        same = ((coarse ^ cp) & 1) == 0
        return jnp.where(same, own[rows, :].astype(F32), other[rows, :].astype(F32))

    parts = []
    for s in range(8):
        x = pick(gl[0, s], 128, 16)
        parts += [x.astype(BF), pltpu.roll(x, 64, 1).astype(BF)]
    gf = dot(zg[...], jnp.concatenate(parts, axis=0), 1, 0).astype(BF)
    parts = []
    for s in range(16):
        d = dl[0, s]
        x = pick(d >> 3, ((d & 7) >> 1) * 32, 32)
        parts.append(jnp.where((d & 1) == 1, pltpu.roll(x, 64, 1), x).astype(BF))
    df = dot(zd[...], jnp.concatenate(parts, axis=0), 1, 0) + dot(dt[...], gf, 1, 0)
    nds[...] = dot(nt[...], df.astype(BF), 1, 0)
    mask = diagonal_mask()
    for n in range(8):
        nf = (nds[pl.ds(n, 32, stride=8), :] + nfar[n * 32:(n + 1) * 32, :]).astype(BF)
        rows = slice(n * 256, (n + 1) * 256)
        lf = (dot(tl[rows, :32], nf, 1, 0) + far[rows, :]).astype(BF)
        for h in range(2):
            g = 2 * n + h
            lanes = slice(g * 256, (g + 1) * 256)
            bg = b[:, lanes]
            bd = jnp.concatenate([bg, bg, bg, bg], axis=0) * mask
            x = dot(lf[h * 128:(h + 1) * 128, :64], bd, 0, 0)
            out[:, lanes] = (x + near[:, lanes]).astype(BF)


AN = pl.BlockSpec(memory_space=pl.ANY)
HB = pl.BlockSpec(memory_space=pltpu.HBM)
VM = pl.BlockSpec(memory_space=pltpu.VMEM)
SM = pl.BlockSpec(memory_space=pltpu.SMEM)


def shape(dims, dtype=BF):
    return jax.ShapeDtypeStruct(dims, dtype)


def params(mib):
    return pltpu.CompilerParams(vmem_limit_bytes=mib * MB)


def cost(flops, size):
    return pl.CostEstimate(flops=flops, bytes_accessed=size, transcendentals=0)


def body(
    vectors, leaf_basis, near_blocks, near_index, leaf_transfer, node_transfer, device_transfer,
    leaf_lists, leaf_coupling, node_lists, node_coupling, device_lists, device_coupling,
    group_lists, group_coupling,
):
    nt = jnp.transpose(node_transfer, (0, 2, 1)).reshape(256, 32)
    dt = device_transfer.reshape(32, 32)
    pay, cown, nown, ma, mb, tl, faces, near_ix, leaf_ix, node_ix = pl.pallas_call(
        up_kernel,
        out_shape=[
            shape((8, 32, 128)), shape((1024, 128)), shape((128, 128)),
            shape((ROWS1, 128)), shape((ROWS1, 128)), shape((2048, 128)),
            shape((1024, 128)),
            shape((12, 64), jnp.int32), shape((16, 64), jnp.int32), shape((8, 16), jnp.int32),
        ],
        in_specs=[HB] * 8,
        out_specs=[VM] * 10,
        scratch_shapes=[
            pltpu.VMEM((2048, 64), BF), pltpu.VMEM((2048, 128), F32), pltpu.VMEM((256, 128), F32),
            pltpu.VMEM((32, 32, 64), BF), pltpu.VMEM((64, 4096), BF), pltpu.VMEM((32, 4096), BF),
            pltpu.VMEM((256, 32), BF), pltpu.VMEM((32, 32), BF), pltpu.VMEM((12, 64), jnp.int32),
            pltpu.VMEM((16, 64), jnp.int32), pltpu.VMEM((8, 16), jnp.int32),
            pltpu.SemaphoreType.DMA((8,)),
        ],
        compiler_params=params(58),
        cost_estimate=cost(10**6, 10**5),
        name="up_pass",
    )(vectors, leaf_basis, leaf_transfer, nt, dt, near_index, leaf_lists, node_lists.T)

    coarse, leafs = lax.axis_size("coarse"), lax.axis_size("leaf")
    r = lax.all_to_all(pay, "leaf", 0, 0, tiled=True)

    def swap(x, axis, first):
        size = lax.axis_size(axis)
        pairs = [(i, i + 1) for i in range(first, size - 1, 2)]
        return lax.ppermute(x, axis, pairs + [(j, i) for i, j in pairs])

    ra, rb = swap(ma, "coarse", 0), swap(mb, "coarse", 1)

    half = [pltpu.VMEM((2, 2048, 128), F32), pltpu.VMEM((8, 32, 32, 64), BF)]
    za = pl.pallas_call(
        first_layout_kernel,
        out_shape=shape((2048, 256)),
        in_specs=[HB],
        out_specs=VM,
        scratch_shapes=half + [pltpu.SemaphoreType.DMA((4,))],
        compiler_params=params(50),
        cost_estimate=cost(1000, 1000000),
        name="first_layout",
    )(leaf_coupling)
    zb, zn, zd, zg = pl.pallas_call(
        second_layout_kernel,
        out_shape=[shape((2048, 256)), shape((256, 512)), shape((32, 512)), shape((32, 256))],
        in_specs=[HB] * 4,
        out_specs=[VM] * 4,
        scratch_shapes=half + [
            pltpu.VMEM((256, 128), F32), pltpu.VMEM((16, 32, 8, 32), BF),
            pltpu.VMEM((16, 32, 32), BF), pltpu.VMEM((8, 32, 32), BF),
            pltpu.SemaphoreType.DMA((4,)), pltpu.SemaphoreType.DMA((3,)),
        ],
        compiler_params=params(50),
        cost_estimate=cost(1000, 1000000),
        name="second_layout",
    )(
        leaf_coupling, jnp.transpose(node_coupling, (0, 1, 3, 2)),
        device_coupling.reshape(16, 32, 32), group_coupling.reshape(8, 32, 32),
    )

    sa, sb = pl.pallas_call(
        pack_kernel,
        out_shape=[shape((ROWS2, 128))] * 2,
        in_specs=[VM] * 5,
        out_specs=[VM] * 2,
        compiler_params=params(8),
        cost_estimate=cost(1000, 10000000),
        name="halo_pack",
    )(faces, cown, nown, ra, rb)
    qa, qb = swap(sa, "leaf", 0), swap(sb, "leaf", 1)

    y = pl.pallas_call(
        group_kernel,
        out_shape=shape((TAB, 128)),
        in_specs=[VM, AN],
        out_specs=VM,
        compiler_params=params(8),
        cost_estimate=cost(1000, 10**5),
        name="group_sum",
    )(r, za)
    flip = lambda x, bit: lax.ppermute(x, "coarse", [(i, i ^ bit) for i in range(coarse)])

    def join(first, second, after):
        return pl.pallas_call(
            table_kernel,
            out_shape=shape((2 * first.shape[0], 128)),
            in_specs=[VM, VM, AN],
            out_specs=VM,
            compiler_params=params(8),
            cost_estimate=cost(1000, 10**5),
            name="table_join",
        )(first, second, after)


    y = join(y, flip(y, 2), sa)
    y = jnp.concatenate([y, flip(y, 4)], axis=0)
    received = flip(y, 8)

    near = pl.pallas_call(
        near_kernel,
        out_shape=shape((64, 4096), F32),
        in_specs=[AN, VM, VM, VM, VM, VM, HB],
        out_specs=VM,
        scratch_shapes=[
            pltpu.VMEM((144, 64, 128), BF), pltpu.SMEM((12, 64), jnp.int32),
            pltpu.VMEM((8, 768, 512), BF), pltpu.SemaphoreType.DMA((9,)),
        ],
        compiler_params=params(48),
        cost_estimate=cost(1000, 1000000),
        name="near_field",
    )(near_ix, vectors, ra, rb, qa, qb, near_blocks.reshape(768, 4096))


    y = join(y, received, zn)
    received = flip(y, 16)

    far, nfar = pl.pallas_call(
        far_kernel,
        out_shape=[shape((2048, 128), F32), shape((256, 128), F32)],
        in_specs=[AN] * 2 + [VM] * 9,
        out_specs=[VM] * 2,
        scratch_shapes=[
            pltpu.VMEM((256, 32, 128), BF), pltpu.VMEM((72, 32, 128), BF), pltpu.SMEM((16, 64), jnp.int32), pltpu.SMEM((8, 16), jnp.int32),
            pltpu.SemaphoreType.DMA((2,)),
        ],
        compiler_params=params(32),
        cost_estimate=cost(1000, 1000000),
        name="far_field",
    )(leaf_ix, node_ix, cown, nown, ra, rb, qa, qb, za, zb, zn)

    own = join(y, received, near)
    other = flip(own, 1)

    return pl.pallas_call(
        down_kernel,
        out_shape=shape((64, 4096)),
        in_specs=[SM] * 2 + [VM] * 11,
        out_specs=VM,
        scratch_shapes=[pltpu.VMEM((256, 128), F32)],
        compiler_params=params(32),
        cost_estimate=cost(10**6, 10**5),
        name="down_pass",
    )(
        device_lists.reshape(1, 16), group_lists.reshape(1, 8), own, other, zd, zg, dt, nt, tl,
        leaf_basis, far, nfar, near,
    )


def solution(mesh):
    both = ("coarse", "leaf")
    placed = (
        P(None, both), P(None, both), P(None, None, both), P(None, both), P(None, None, both),
        P(None, None, both), P(None, None, both), P(None, both), P(None, None, None, both),
        P(None, both), P(None, None, None, both), P(None, both), P(None, None, None, both),
        P(None, "coarse"), P(None, None, None, "coarse"),
    )
    return jax.shard_map(
        body, mesh=mesh, in_specs=placed, out_specs=P(None, both), check_vma=False
    )
```

```python
import jax
import jax.numpy as jnp
from jax import lax
from jax.experimental import pallas as pl
from jax.experimental.pallas import tpu as pltpu
from jax.sharding import PartitionSpec as P

BF = jnp.bfloat16
F32 = jnp.float32
V1, C1, N1 = 512, 512, 128
V2, C2, N2 = 768, 1024, 384
ROWS1 = V1 + C1 + N1
ROWS2 = V2 + C2 + N2
TAB = 144
MB = 1024 * 1024


def dot(a, b, ca, cb):
    return lax.dot_general(a, b, (((ca,), (cb,)), ((), ())), preferred_element_type=F32)


def copies(pairs, sems):
    started = [pltpu.make_async_copy(src, dst, sems.at[i]) for i, (src, dst) in enumerate(pairs)]
    for c in started:
        c.start()
    return started


def eye(n):
    rows = lax.broadcasted_iota(jnp.int32, (n, n), 0)
    cols = lax.broadcasted_iota(jnp.int32, (n, n), 1)
    return jnp.where(rows == cols, 1.0, 0.0).astype(BF)


def diagonal_mask():
    rows = lax.broadcasted_iota(jnp.int32, (128, 256), 0)
    cols = lax.broadcasted_iota(jnp.int32, (128, 256), 1)
    return jnp.where((rows >> 5) == (cols >> 6), 1.0, 0.0).astype(BF)


def low_lanes(rows):
    return lax.broadcasted_iota(jnp.int32, (rows, 128), 1) < 64


def node_parts(node):
    block, rest = node >> 3, node & 7
    return 2 * (block >> 3) + (rest >> 2), 2 * (block & 7) + ((rest >> 1) & 1), rest & 1


def up_kernel(
    v_hbm, b_hbm, lt_hbm, nt_hbm, dt_hbm, near_hbm, leaf_hbm, node_hbm,
    pay, cown, nown, ma, mb, tl, faces, near_ix, leaf_ix, node_ix,
    ct, tls, ncs, lt, v, b, nt, dt, near_in, leaf_in, node_in, sems,
):
    loads = copies(
        [
            (lt_hbm, lt), (v_hbm, v), (b_hbm, b), (nt_hbm, nt), (dt_hbm, dt),
            (near_hbm, near_in), (leaf_hbm, leaf_in), (node_hbm, node_in),
        ],
        sems,
    )
    ident = eye(64)
    loads[0].wait()
    for q in range(8):
        t = dot(ident, lt[4 * q:4 * q + 4].reshape(128, 64), 1, 1)
        for i in range(4):
            tls[pl.ds(4 * q + i, 64, stride=32), :] = pltpu.roll(t, (128 - 32 * i) % 128, 1) if i else t
    tl[...] = tls[...].astype(BF)
    for c in loads[1:]:
        c.wait()
    cp, lp = lax.axis_index("coarse"), lax.axis_index("leaf")
    num = near_in[...]
    px, py, pz = node_parts(num >> 3)
    lx = 2 * px + ((num >> 2) & 1) - 4 * cp + 1
    ly = 2 * py + ((num >> 1) & 1) - 4 * lp + 1
    near_ix[...] = jnp.clip((lx * 6 + ly) * 4 + 2 * pz + (num & 1), 0, 143)
    num = leaf_in[...]
    px, py, pz = node_parts(num >> 3)
    at = ((px - 2 * cp + 1) * 4 + (py - 2 * lp + 1)) * 2 + pz
    leaf_ix[...] = jnp.clip(at * 8 + (num & 7), 0, 255)
    px, py, pz = node_parts(node_in[...])
    at = ((px - 2 * cp + 2) * 6 + (py - 2 * lp + 2)) * 2 + pz
    node_ix[...] = jnp.clip(at, 0, 71)
    mask = diagonal_mask()
    for g in range(16):
        lanes = slice(g * 256, (g + 1) * 256)
        bg = b[:, lanes]
        bd = jnp.concatenate([bg, bg, bg, bg], axis=0) * mask
        c = dot(bd, v[:, lanes], 1, 1)
        ct[g * 128:(g + 1) * 128, :] = c.astype(BF)
        for h in range(2):
            pair = jnp.concatenate([c[h * 64:h * 64 + 32], c[h * 64 + 32:h * 64 + 64]], axis=1)
            cown[(2 * g + h) * 32:(2 * g + h + 1) * 32, :] = pair.astype(BF)
    for m in range(4):
        parts = []
        for n in (2 * m, 2 * m + 1):
            rows = slice(n * 256, (n + 1) * 256)
            nc = dot(tl[rows, :32], ct[rows, :], 0, 0)
            parts.append(nc)
            wide = jnp.concatenate([nc, nc], axis=1)
            ncs[pl.ds(n, 32, stride=8), :] = wide.astype(BF).astype(F32)
        nown[m * 32:(m + 1) * 32, :] = jnp.concatenate(parts, axis=1).astype(BF)
    dc = dot(nt[...], ncs[...].astype(BF), 0, 0)
    terms = dot(dt[...], dc.astype(BF), 0, 0)
    message = jnp.where(low_lanes(32), dc, terms).astype(BF)
    for z in range(8):
        pay[z] = message
    for out, side in ((ma, 1 - (cp & 1)), (mb, cp & 1)):
        for j in range(2):
            for k in range(2):
                for bb in range(2):
                    at = ((2 * j + k) * 2 + bb) * 64
                    first = ((2 * j + k) * 8 + 2 * bb) * 64 + side * 2304
                    out[at:at + 64, :] = v[:, pl.ds(pl.multiple_of(first, 128), 128)]
        out[V1:V1 + C1, :] = cown[pl.ds(pl.multiple_of(side * 512, 512), 512), :]
        out[V1 + C1:, :] = nown[...]
    for j in range(2):
        for i in range(2):
            for a in range(2):
                for k in range(2):
                    at = j * 512 + ((i * 2 + a) * 2 + k) * 64
                    first = ((i * 4 + k) * 8 + 4 * a + 18 * j) * 64
                    faces[at:at + 64, :] = v[:, first:first + 128]


def pack_kernel(faces, cown, nown, ra, rb, qa, qb):
    lp = lax.axis_index("leaf")
    for out, j in ((qa, 1 - (lp & 1)), (qb, lp & 1)):
        rows = [(faces, j * 512, 512)]
        for side in (ra, rb):
            rows += [(side, (5 * j + 2 * k) * 64, 64) for k in range(2)]
        rows += [(cown, (i * 2 + j) * 256, 256) for i in range(2)]
        rows += [(side, V1 + j * 256, 256) for side in (ra, rb)]
        rows += [(nown, 0, 128), (ra, V1 + C1, 128), (rb, V1 + C1, 128)]
        at = 0
        for side, first, count in rows:
            if not isinstance(first, int):
                first = pl.multiple_of(first, 64)
            out[at:at + count, :] = side[pl.ds(first, count), :]
            at += count


def group_kernel(r, after, y):
    low = low_lanes(32)
    total = jnp.zeros((32, 128), F32)
    for m in range(4):
        lo, hi = r[2 * m].astype(F32), r[2 * m + 1].astype(F32)
        total = total + lo + hi
        y[m * 32:(m + 1) * 32, :] = jnp.where(low, lo, pltpu.roll(hi, 64, 1)).astype(BF)
    swapped = pltpu.roll(total, 64, 1)
    y[128:144, :] = jnp.where(low_lanes(16), swapped[0:16], total[16:32]).astype(BF)


def transpose_half(base, s_hbm, zl, zs, s, sems):
    loads = copies(
        [
            (s_hbm.at[pl.ds(base, 8), pl.ds(8 * q, 8)], s.at[:, pl.ds(8 * q, 8)])
            for q in range(4)
        ],
        sems,
    )
    ident = eye(64)
    for j in range(32):
        if j % 8 == 0:
            loads[j // 8].wait()
        x = s[:, j].reshape(256, 64)
        t = dot(ident, x, 1, 1) if j % 2 else x.T.astype(F32)
        for q in range(2):
            zs[q, pl.ds(j, 64, stride=32), :] = t[:, q * 128:(q + 1) * 128]
    for q in range(2):
        zl[:, q * 128:(q + 1) * 128] = zs[q].astype(BF)


def first_layout_kernel(s_hbm, zl, zs, s, sems):
    transpose_half(0, s_hbm, zl, zs, s, sems)


def second_layout_kernel(
    s_hbm, sn_hbm, sd_hbm, sg_hbm, zl, zn, zd, zg, zs, s, ns, sn, sd, sg, sems, more
):
    loads = copies([(sn_hbm, sn), (sd_hbm, sd), (sg_hbm, sg)], more)
    transpose_half(8, s_hbm, zl, zs, s, sems)
    for c in loads:
        c.wait()
    for q in range(4):
        parts = [sn[4 * q + i].astype(F32).reshape(256, 32) for i in range(4)]
        ns[...] = jnp.concatenate(parts, axis=1)
        for n in range(8):
            zn[n * 32:(n + 1) * 32, q * 128:(q + 1) * 128] = ns[pl.ds(n, 32, stride=8), :].astype(BF)
        parts = [sd[4 * q + i].astype(F32) for i in range(4)]
        zd[:, q * 128:(q + 1) * 128] = jnp.concatenate(parts, axis=1).astype(BF)
    for q in range(2):
        parts = [sg[4 * q + i].astype(F32) for i in range(4)]
        zg[:, q * 128:(q + 1) * 128] = jnp.concatenate(parts, axis=1).astype(BF)


def near_kernel(ix_any, v, ra, rb, qa, qb, blocks_hbm, out, pieces, ix, blocks, sems):
    loads = copies(
        [(ix_any, ix)]
        + [(blocks_hbm.at[:, pl.ds(512 * t, 512)], blocks.at[t]) for t in range(8)],
        sems,
    )
    mask = low_lanes(64)
    odd_c, odd_l = lax.axis_index("coarse") & 1, lax.axis_index("leaf") & 1

    def table():
        def put(wx, wy, k, x):
            at = (wx * 6 + wy) * 4 + 2 * k
            pieces[at] = x
            pieces[at + 1] = pltpu.roll(x.astype(F32), 64, 1).astype(BF)

        for i in range(2):
            for j in range(2):
                for k in range(2):
                    for a in range(2):
                        for bb in range(2):
                            first = (((i * 2 + j) * 2 + k) * 8 + 4 * a + 2 * bb) * 64
                            put(1 + 2 * i + a, 1 + 2 * j + bb, k, v[:, first:first + 128])
        for side, wx in ((ra, 5 - 5 * odd_c), (rb, 5 * odd_c)):
            for j in range(2):
                for k in range(2):
                    for bb in range(2):
                        first = ((2 * j + k) * 2 + bb) * 64
                        put(wx, 1 + 2 * j + bb, k, side[first:first + 64, :])
        for side, wy in ((qa, 5 - 5 * odd_l), (qb, 5 * odd_l)):
            for i in range(2):
                for a in range(2):
                    for k in range(2):
                        first = ((i * 2 + a) * 2 + k) * 64
                        put(1 + 2 * i + a, wy, k, side[first:first + 64, :])
            for wx, base in ((5 - 5 * odd_c, 8), (5 * odd_c, 10)):
                for k in range(2):
                    first = (base + k) * 64
                    put(wx, wy, k, side[first:first + 64, :])

    table()
    loads[0].wait()

    def chunk(t, carry):
        pltpu.make_async_copy(
            blocks_hbm.at[:, pl.ds(pl.multiple_of(512 * t, 512), 512)], blocks.at[t], sems.at[t + 1]
        ).wait()
        for q in range(4):
            lhs = []
            for i in range(2):
                leaf = t * 8 + 2 * q + i
                lhs.append(jnp.concatenate(
                    [
                        jnp.where(mask, pieces[ix[2 * sp, leaf]], pieces[ix[2 * sp + 1, leaf] ^ 1])
                        for sp in range(6)
                    ],
                    axis=1,
                ))
            r = dot(jnp.concatenate(lhs, axis=0), blocks[t, :, q * 128:(q + 1) * 128], 1, 0)
            lanes = pl.ds(pl.multiple_of(t * 512 + q * 128, 128), 128)
            out[:, lanes] = jnp.where(mask, r[:64], r[64:])
        return carry

    lax.fori_loop(0, 8, chunk, 0, unroll=2)


def far_kernel(
    li_any, mi_any, cown, nown, ra, rb, qa, qb, za, zb, zn, far, nfar, pieces, nw, li, mi, sems
):
    loads = copies([(li_any, li), (mi_any, mi)], sems)
    mask = low_lanes(32)

    def put_leaves(nwx, nwy, k, side, first):
        for p in range(4):
            x = side[first + p * 32:first + (p + 1) * 32, :]
            at = ((nwx * 4 + nwy) * 2 + k) * 8 + 2 * p
            pieces[at] = x
            pieces[at + 1] = pltpu.roll(x.astype(F32), 64, 1).astype(BF)

    def put_nodes(nwx, nwy, side, first):
        x = side[first:first + 32, :]
        at = (nwx * 6 + nwy) * 2
        nw[at] = x
        nw[at + 1] = pltpu.roll(x.astype(F32), 64, 1).astype(BF)

    odd_c, odd_l = lax.axis_index("coarse") & 1, lax.axis_index("leaf") & 1
    in_x, in_y = ((ra, 1 - odd_c), (rb, odd_c)), ((qa, 1 - odd_l), (qb, odd_l))
    for i in range(2):
        for j in range(2):
            put_nodes(2 + i, 2 + j, nown, (i * 2 + j) * 32)
            for side, after in in_x:
                put_nodes(4 * after + i, 2 + j, side, V1 + C1 + (i * 2 + j) * 32)
            for side, after in in_y:
                first = V2 + C2 + (i * 2 + j) * 32
                put_nodes(2 + i, 4 * after + j, side, first)
                put_nodes(4 - 4 * odd_c + i, 4 * after + j, side, first + 128)
                put_nodes(4 * odd_c + i, 4 * after + j, side, first + 256)
            for k in range(2):
                put_leaves(1 + i, 1 + j, k, cown, ((i * 2 + j) * 2 + k) * 128)
    for j in range(2):
        for k in range(2):
            for side, after in in_x:
                put_leaves(3 * after, 1 + j, k, side, V1 + (2 * j + k) * 128)
    for side, after in in_y:
        for k in range(2):
            for i in range(2):
                put_leaves(1 + i, 3 * after, k, side, V2 + (2 * i + k) * 128)
            put_leaves(3 - 3 * odd_c, 3 * after, k, side, V2 + 512 + k * 128)
            put_leaves(3 * odd_c, 3 * after, k, side, V2 + 768 + k * 128)

    for c in loads:
        c.wait()
    for n in range(8):
        block = jnp.concatenate([nw[mi[n, s]] for s in range(16)], axis=0)
        nfar[n * 32:(n + 1) * 32, :] = dot(zn[n * 32:(n + 1) * 32, :], block, 1, 0)

    def leaves(t, carry):
        for u in range(4):
            n = t * 8 + 2 * u
            block = jnp.concatenate(
                [jnp.where(mask, pieces[li[s, n]], pieces[li[s, n + 1] ^ 1]) for s in range(16)],
                axis=0,
            )
            rows = pl.ds(pl.multiple_of(n * 32, 64), 64)
            r = dot(za[rows, :], block[:256], 1, 0) + dot(zb[rows, :], block[256:], 1, 0)
            far[pl.ds(pl.multiple_of(n * 32, 32), 32), :] = r[:32]
            far[pl.ds(pl.multiple_of(n * 32 + 32, 32), 32), :] = pltpu.roll(r[32:], 64, 1)
        return carry

    lax.fori_loop(0, 8, leaves, 0, unroll=8)


def table_kernel(y, received, after, own):
    half = y.shape[0]
    own[0:half, :] = y[...]
    own[half:, :] = received[...]


def down_kernel(
    dl, gl, own, other, zd, zg, dt, nt, tl, b, far, nfar, near, out_hbm, nds, out, sems
):
    cp = lax.axis_index("coarse")

    def pick(coarse, row, count):
        at = (coarse ^ cp) >> 1
        rows = pl.ds(pl.multiple_of(at * TAB + row, 16), count)
        same = ((coarse ^ cp) & 1) == 0
        return jnp.where(same, own[rows, :].astype(F32), other[rows, :].astype(F32))

    parts = []
    for s in range(8):
        x = pick(gl[0, s], 128, 16)
        parts += [x.astype(BF), pltpu.roll(x, 64, 1).astype(BF)]
    gf = dot(zg[...], jnp.concatenate(parts, axis=0), 1, 0).astype(BF)
    parts = []
    for s in range(16):
        d = dl[0, s]
        x = pick(d >> 3, ((d & 7) >> 1) * 32, 32)
        parts.append(jnp.where((d & 1) == 1, pltpu.roll(x, 64, 1), x).astype(BF))
    df = dot(zd[...], jnp.concatenate(parts, axis=0), 1, 0) + dot(dt[...], gf, 1, 0)
    nds[...] = dot(nt[...], df.astype(BF), 1, 0)
    mask = diagonal_mask()
    for n in range(8):
        nf = (nds[pl.ds(n, 32, stride=8), :] + nfar[n * 32:(n + 1) * 32, :]).astype(BF)
        rows = slice(n * 256, (n + 1) * 256)
        lf = (dot(tl[rows, :32], nf, 1, 0) + far[rows, :]).astype(BF)
        for h in range(2):
            g = 2 * n + h
            lanes = slice(g * 256, (g + 1) * 256)
            bg = b[:, lanes]
            bd = jnp.concatenate([bg, bg, bg, bg], axis=0) * mask
            x = dot(lf[h * 128:(h + 1) * 128, :64], bd, 0, 0)
            out[:, lanes] = (x + near[:, lanes]).astype(BF)
        lanes = pl.ds(n * 512, 512)
        pltpu.make_async_copy(out.at[:, lanes], out_hbm.at[:, lanes], sems.at[n]).start()
    for n in range(8):
        lanes = pl.ds(n * 512, 512)
        pltpu.make_async_copy(out.at[:, lanes], out_hbm.at[:, lanes], sems.at[n]).wait()


AN = pl.BlockSpec(memory_space=pl.ANY)
HB = pl.BlockSpec(memory_space=pltpu.HBM)
VM = pl.BlockSpec(memory_space=pltpu.VMEM)
SM = pl.BlockSpec(memory_space=pltpu.SMEM)


def shape(dims, dtype=BF):
    return jax.ShapeDtypeStruct(dims, dtype)


def params(mib):
    return pltpu.CompilerParams(vmem_limit_bytes=mib * MB)


def cost(flops, size):
    return pl.CostEstimate(flops=flops, bytes_accessed=size, transcendentals=0)


def body(
    vectors, leaf_basis, near_blocks, near_index, leaf_transfer, node_transfer, device_transfer,
    leaf_lists, leaf_coupling, node_lists, node_coupling, device_lists, device_coupling,
    group_lists, group_coupling,
):
    nt = jnp.transpose(node_transfer, (0, 2, 1)).reshape(256, 32)
    dt = device_transfer.reshape(32, 32)
    pay, cown, nown, ma, mb, tl, faces, near_ix, leaf_ix, node_ix = pl.pallas_call(
        up_kernel,
        out_shape=[
            shape((8, 32, 128)), shape((1024, 128)), shape((128, 128)),
            shape((ROWS1, 128)), shape((ROWS1, 128)), shape((2048, 128)),
            shape((1024, 128)),
            shape((12, 64), jnp.int32), shape((16, 64), jnp.int32), shape((8, 16), jnp.int32),
        ],
        in_specs=[HB] * 8,
        out_specs=[VM] * 10,
        scratch_shapes=[
            pltpu.VMEM((2048, 64), BF), pltpu.VMEM((2048, 128), F32), pltpu.VMEM((256, 128), F32),
            pltpu.VMEM((32, 32, 64), BF), pltpu.VMEM((64, 4096), BF), pltpu.VMEM((32, 4096), BF),
            pltpu.VMEM((256, 32), BF), pltpu.VMEM((32, 32), BF), pltpu.VMEM((12, 64), jnp.int32),
            pltpu.VMEM((16, 64), jnp.int32), pltpu.VMEM((8, 16), jnp.int32),
            pltpu.SemaphoreType.DMA((8,)),
        ],
        compiler_params=params(58),
        cost_estimate=cost(10**6, 10**5),
        name="up_pass",
    )(vectors, leaf_basis, leaf_transfer, nt, dt, near_index, leaf_lists, node_lists.T)

    coarse, leafs = lax.axis_size("coarse"), lax.axis_size("leaf")
    r = lax.all_to_all(pay, "leaf", 0, 0, tiled=True)

    def swap(x, axis, first):
        size = lax.axis_size(axis)
        pairs = [(i, i + 1) for i in range(first, size - 1, 2)]
        return lax.ppermute(x, axis, pairs + [(j, i) for i, j in pairs])

    ra, rb = swap(ma, "coarse", 0), swap(mb, "coarse", 1)

    half = [pltpu.VMEM((2, 2048, 128), F32), pltpu.VMEM((8, 32, 32, 64), BF)]
    za = pl.pallas_call(
        first_layout_kernel,
        out_shape=shape((2048, 256)),
        in_specs=[HB],
        out_specs=VM,
        scratch_shapes=half + [pltpu.SemaphoreType.DMA((4,))],
        compiler_params=params(50),
        cost_estimate=cost(1000, 1000000),
        name="first_layout",
    )(leaf_coupling)
    zb, zn, zd, zg = pl.pallas_call(
        second_layout_kernel,
        out_shape=[shape((2048, 256)), shape((256, 512)), shape((32, 512)), shape((32, 256))],
        in_specs=[HB] * 4,
        out_specs=[VM] * 4,
        scratch_shapes=half + [
            pltpu.VMEM((256, 128), F32), pltpu.VMEM((16, 32, 8, 32), BF),
            pltpu.VMEM((16, 32, 32), BF), pltpu.VMEM((8, 32, 32), BF),
            pltpu.SemaphoreType.DMA((4,)), pltpu.SemaphoreType.DMA((3,)),
        ],
        compiler_params=params(50),
        cost_estimate=cost(1000, 1000000),
        name="second_layout",
    )(
        leaf_coupling, jnp.transpose(node_coupling, (0, 1, 3, 2)),
        device_coupling.reshape(16, 32, 32), group_coupling.reshape(8, 32, 32),
    )

    sa, sb = pl.pallas_call(
        pack_kernel,
        out_shape=[shape((ROWS2, 128))] * 2,
        in_specs=[VM] * 5,
        out_specs=[VM] * 2,
        compiler_params=params(8),
        cost_estimate=cost(1000, 10000000),
        name="halo_pack",
    )(faces, cown, nown, ra, rb)
    qa, qb = swap(sa, "leaf", 0), swap(sb, "leaf", 1)

    y = pl.pallas_call(
        group_kernel,
        out_shape=shape((TAB, 128)),
        in_specs=[VM, AN],
        out_specs=VM,
        compiler_params=params(8),
        cost_estimate=cost(1000, 10**5),
        name="group_sum",
    )(r, za)
    flip = lambda x, bit: lax.ppermute(x, "coarse", [(i, i ^ bit) for i in range(coarse)])

    def join(first, second, after):
        return pl.pallas_call(
            table_kernel,
            out_shape=shape((2 * first.shape[0], 128)),
            in_specs=[VM, VM, AN],
            out_specs=VM,
            compiler_params=params(8),
            cost_estimate=cost(1000, 10**5),
            name="table_join",
        )(first, second, after)


    y = join(y, flip(y, 2), sa)
    y = jnp.concatenate([y, flip(y, 4)], axis=0)
    received = flip(y, 8)

    near = pl.pallas_call(
        near_kernel,
        out_shape=shape((64, 4096), F32),
        in_specs=[AN, VM, VM, VM, VM, VM, HB],
        out_specs=VM,
        scratch_shapes=[
            pltpu.VMEM((144, 64, 128), BF), pltpu.SMEM((12, 64), jnp.int32),
            pltpu.VMEM((8, 768, 512), BF), pltpu.SemaphoreType.DMA((9,)),
        ],
        compiler_params=params(48),
        cost_estimate=cost(1000, 1000000),
        name="near_field",
    )(near_ix, vectors, ra, rb, qa, qb, near_blocks.reshape(768, 4096))


    y = join(y, received, zn)
    received = flip(y, 16)

    far, nfar = pl.pallas_call(
        far_kernel,
        out_shape=[shape((2048, 128), F32), shape((256, 128), F32)],
        in_specs=[AN] * 2 + [VM] * 9,
        out_specs=[VM] * 2,
        scratch_shapes=[
            pltpu.VMEM((256, 32, 128), BF), pltpu.VMEM((72, 32, 128), BF), pltpu.SMEM((16, 64), jnp.int32), pltpu.SMEM((8, 16), jnp.int32),
            pltpu.SemaphoreType.DMA((2,)),
        ],
        compiler_params=params(32),
        cost_estimate=cost(1000, 1000000),
        name="far_field",
    )(leaf_ix, node_ix, cown, nown, ra, rb, qa, qb, za, zb, zn)

    own = join(y, received, near)
    other = flip(own, 1)

    return pl.pallas_call(
        down_kernel,
        out_shape=shape((64, 4096)),
        in_specs=[SM] * 2 + [VM] * 11,
        out_specs=HB,
        scratch_shapes=[
            pltpu.VMEM((256, 128), F32), pltpu.VMEM((64, 4096), BF), pltpu.SemaphoreType.DMA((8,)),
        ],
        compiler_params=params(32),
        cost_estimate=cost(10**6, 10**5),
        name="down_pass",
    )(
        device_lists.reshape(1, 16), group_lists.reshape(1, 8), own, other, zd, zg, dt, nt, tl,
        leaf_basis, far, nfar, near,
    )


def solution(mesh):
    both = ("coarse", "leaf")
    placed = (
        P(None, both), P(None, both), P(None, None, both), P(None, both), P(None, None, both),
        P(None, None, both), P(None, None, both), P(None, both), P(None, None, None, both),
        P(None, both), P(None, None, None, both), P(None, both), P(None, None, None, both),
        P(None, "coarse"), P(None, None, None, "coarse"),
    )
    return jax.shard_map(
        body, mesh=mesh, in_specs=placed, out_specs=P(None, both), check_vma=False
    )
```

```python
import jax
import jax.numpy as jnp
from jax import lax
from jax.experimental import pallas as pl
from jax.experimental.pallas import tpu as pltpu
from jax.sharding import PartitionSpec as P

BF = jnp.bfloat16
F32 = jnp.float32
V1, C1, N1 = 512, 512, 128
V2, C2, N2 = 768, 1024, 384
ROWS1 = V1 + C1 + N1
ROWS2 = V2 + C2 + N2
TAB = 144
MB = 1024 * 1024


def dot(a, b, ca, cb):
    return lax.dot_general(a, b, (((ca,), (cb,)), ((), ())), preferred_element_type=F32)


def copies(pairs, sems):
    started = [pltpu.make_async_copy(src, dst, sems.at[i]) for i, (src, dst) in enumerate(pairs)]
    for c in started:
        c.start()
    return started


def eye(n):
    rows = lax.broadcasted_iota(jnp.int32, (n, n), 0)
    cols = lax.broadcasted_iota(jnp.int32, (n, n), 1)
    return jnp.where(rows == cols, 1.0, 0.0).astype(BF)


def diagonal_mask():
    rows = lax.broadcasted_iota(jnp.int32, (128, 256), 0)
    cols = lax.broadcasted_iota(jnp.int32, (128, 256), 1)
    return jnp.where((rows >> 5) == (cols >> 6), 1.0, 0.0).astype(BF)


def low_lanes(rows):
    return lax.broadcasted_iota(jnp.int32, (rows, 128), 1) < 64


def node_parts(node):
    block, rest = node >> 3, node & 7
    return 2 * (block >> 3) + (rest >> 2), 2 * (block & 7) + ((rest >> 1) & 1), rest & 1


def up_kernel(
    v_hbm, b_hbm, lt_hbm, nt_hbm, dt_hbm, near_hbm, leaf_hbm, node_hbm,
    pay, cown, nown, ma, mb, tl, faces, near_ix, leaf_ix, node_ix,
    ct, tls, ncs, lt, v, b, nt, dt, near_in, leaf_in, node_in, sems,
):
    loads = copies(
        [
            (lt_hbm, lt), (v_hbm, v), (b_hbm, b), (nt_hbm, nt), (dt_hbm, dt),
            (near_hbm, near_in), (leaf_hbm, leaf_in), (node_hbm, node_in),
        ],
        sems,
    )
    ident = eye(64)
    loads[0].wait()
    for q in range(8):
        t = dot(ident, lt[4 * q:4 * q + 4].reshape(128, 64), 1, 1)
        for i in range(4):
            tls[pl.ds(4 * q + i, 64, stride=32), :] = pltpu.roll(t, (128 - 32 * i) % 128, 1) if i else t
    tl[...] = tls[...].astype(BF)
    for c in loads[1:]:
        c.wait()
    cp, lp = lax.axis_index("coarse"), lax.axis_index("leaf")
    num = near_in[...]
    px, py, pz = node_parts(num >> 3)
    lx = 2 * px + ((num >> 2) & 1) - 4 * cp + 1
    ly = 2 * py + ((num >> 1) & 1) - 4 * lp + 1
    near_ix[...] = jnp.clip((lx * 6 + ly) * 4 + 2 * pz + (num & 1), 0, 143)
    num = leaf_in[...]
    px, py, pz = node_parts(num >> 3)
    at = ((px - 2 * cp + 1) * 4 + (py - 2 * lp + 1)) * 2 + pz
    leaf_ix[...] = jnp.clip(at * 8 + (num & 7), 0, 255)
    px, py, pz = node_parts(node_in[...])
    at = ((px - 2 * cp + 2) * 6 + (py - 2 * lp + 2)) * 2 + pz
    node_ix[...] = jnp.clip(at, 0, 71)
    mask = diagonal_mask()
    for g in range(16):
        lanes = slice(g * 256, (g + 1) * 256)
        bg = b[:, lanes]
        bd = jnp.concatenate([bg, bg, bg, bg], axis=0) * mask
        c = dot(bd, v[:, lanes], 1, 1)
        ct[g * 128:(g + 1) * 128, :] = c.astype(BF)
        for h in range(2):
            pair = jnp.concatenate([c[h * 64:h * 64 + 32], c[h * 64 + 32:h * 64 + 64]], axis=1)
            cown[(2 * g + h) * 32:(2 * g + h + 1) * 32, :] = pair.astype(BF)
    for m in range(4):
        parts = []
        for n in (2 * m, 2 * m + 1):
            rows = slice(n * 256, (n + 1) * 256)
            nc = dot(tl[rows, :32], ct[rows, :], 0, 0)
            parts.append(nc)
            wide = jnp.concatenate([nc, nc], axis=1)
            ncs[pl.ds(n, 32, stride=8), :] = wide.astype(BF).astype(F32)
        nown[m * 32:(m + 1) * 32, :] = jnp.concatenate(parts, axis=1).astype(BF)
    dc = dot(nt[...], ncs[...].astype(BF), 0, 0)
    terms = dot(dt[...], dc.astype(BF), 0, 0)
    message = jnp.where(low_lanes(32), dc, terms).astype(BF)
    for z in range(8):
        pay[z] = message
    for out, side in ((ma, 1 - (cp & 1)), (mb, cp & 1)):
        for j in range(2):
            for k in range(2):
                for bb in range(2):
                    at = ((2 * j + k) * 2 + bb) * 64
                    first = ((2 * j + k) * 8 + 2 * bb) * 64 + side * 2304
                    out[at:at + 64, :] = v[:, pl.ds(pl.multiple_of(first, 128), 128)]
        out[V1:V1 + C1, :] = cown[pl.ds(pl.multiple_of(side * 512, 512), 512), :]
        out[V1 + C1:, :] = nown[...]
    for j in range(2):
        for i in range(2):
            for a in range(2):
                for k in range(2):
                    at = j * 512 + ((i * 2 + a) * 2 + k) * 64
                    first = ((i * 4 + k) * 8 + 4 * a + 18 * j) * 64
                    faces[at:at + 64, :] = v[:, first:first + 128]


def pack_kernel(faces, cown, nown, ra, rb, qa, qb):
    lp = lax.axis_index("leaf")
    for out, j in ((qa, 1 - (lp & 1)), (qb, lp & 1)):
        rows = [(faces, j * 512, 512)]
        for side in (ra, rb):
            rows += [(side, (5 * j + 2 * k) * 64, 64) for k in range(2)]
        rows += [(cown, (i * 2 + j) * 256, 256) for i in range(2)]
        rows += [(side, V1 + j * 256, 256) for side in (ra, rb)]
        rows += [(nown, 0, 128), (ra, V1 + C1, 128), (rb, V1 + C1, 128)]
        at = 0
        for side, first, count in rows:
            if not isinstance(first, int):
                first = pl.multiple_of(first, 64)
            out[at:at + count, :] = side[pl.ds(first, count), :]
            at += count


def group_kernel(r, after, y):
    low = low_lanes(32)
    total = jnp.zeros((32, 128), F32)
    for m in range(4):
        lo, hi = r[2 * m].astype(F32), r[2 * m + 1].astype(F32)
        total = total + lo + hi
        y[m * 32:(m + 1) * 32, :] = jnp.where(low, lo, pltpu.roll(hi, 64, 1)).astype(BF)
    swapped = pltpu.roll(total, 64, 1)
    y[128:144, :] = jnp.where(low_lanes(16), swapped[0:16], total[16:32]).astype(BF)


def transpose_half(base, s_hbm, zl, zs, s, sems):
    loads = copies(
        [
            (s_hbm.at[pl.ds(base, 8), pl.ds(8 * q, 8)], s.at[:, pl.ds(8 * q, 8)])
            for q in range(4)
        ],
        sems,
    )
    ident = eye(64)
    for j in range(32):
        if j % 8 == 0:
            loads[j // 8].wait()
        x = s[:, j].reshape(256, 64)
        t = dot(ident, x, 1, 1) if j % 2 else x.T.astype(F32)
        for q in range(2):
            zs[q, pl.ds(j, 64, stride=32), :] = t[:, q * 128:(q + 1) * 128]
    for q in range(2):
        zl[:, q * 128:(q + 1) * 128] = zs[q].astype(BF)


def first_layout_kernel(s_hbm, zl, zs, s, sems):
    transpose_half(0, s_hbm, zl, zs, s, sems)


def second_layout_kernel(
    s_hbm, sn_hbm, sd_hbm, sg_hbm, zl, zn, zd, zg, zs, s, ns, sn, sd, sg, sems, more
):
    loads = copies([(sn_hbm, sn), (sd_hbm, sd), (sg_hbm, sg)], more)
    transpose_half(8, s_hbm, zl, zs, s, sems)
    for c in loads:
        c.wait()
    for q in range(4):
        parts = [sn[4 * q + i].astype(F32).reshape(256, 32) for i in range(4)]
        ns[...] = jnp.concatenate(parts, axis=1)
        for n in range(8):
            zn[n * 32:(n + 1) * 32, q * 128:(q + 1) * 128] = ns[pl.ds(n, 32, stride=8), :].astype(BF)
        parts = [sd[4 * q + i].astype(F32) for i in range(4)]
        zd[:, q * 128:(q + 1) * 128] = jnp.concatenate(parts, axis=1).astype(BF)
    for q in range(2):
        parts = [sg[4 * q + i].astype(F32) for i in range(4)]
        zg[:, q * 128:(q + 1) * 128] = jnp.concatenate(parts, axis=1).astype(BF)


def near_kernel(ix_any, v, ra, rb, qa, qb, blocks_hbm, out, pieces, ix, blocks, sems):
    loads = copies(
        [(ix_any, ix)]
        + [(blocks_hbm.at[:, pl.ds(512 * t, 512)], blocks.at[t]) for t in range(8)],
        sems,
    )
    mask = low_lanes(64)
    odd_c, odd_l = lax.axis_index("coarse") & 1, lax.axis_index("leaf") & 1

    def table():
        def put(wx, wy, k, x):
            at = (wx * 6 + wy) * 4 + 2 * k
            pieces[at] = x
            pieces[at + 1] = pltpu.roll(x.astype(F32), 64, 1).astype(BF)

        for i in range(2):
            for j in range(2):
                for k in range(2):
                    for a in range(2):
                        for bb in range(2):
                            first = (((i * 2 + j) * 2 + k) * 8 + 4 * a + 2 * bb) * 64
                            put(1 + 2 * i + a, 1 + 2 * j + bb, k, v[:, first:first + 128])
        for side, wx in ((ra, 5 - 5 * odd_c), (rb, 5 * odd_c)):
            for j in range(2):
                for k in range(2):
                    for bb in range(2):
                        first = ((2 * j + k) * 2 + bb) * 64
                        put(wx, 1 + 2 * j + bb, k, side[first:first + 64, :])
        for side, wy in ((qa, 5 - 5 * odd_l), (qb, 5 * odd_l)):
            for i in range(2):
                for a in range(2):
                    for k in range(2):
                        first = ((i * 2 + a) * 2 + k) * 64
                        put(1 + 2 * i + a, wy, k, side[first:first + 64, :])
            for wx, base in ((5 - 5 * odd_c, 8), (5 * odd_c, 10)):
                for k in range(2):
                    first = (base + k) * 64
                    put(wx, wy, k, side[first:first + 64, :])

    table()
    loads[0].wait()

    def chunk(t, carry):
        pltpu.make_async_copy(
            blocks_hbm.at[:, pl.ds(pl.multiple_of(512 * t, 512), 512)], blocks.at[t], sems.at[t + 1]
        ).wait()
        for q in range(4):
            lhs = []
            for i in range(2):
                leaf = t * 8 + 2 * q + i
                lhs.append(jnp.concatenate(
                    [
                        jnp.where(mask, pieces[ix[2 * sp, leaf]], pieces[ix[2 * sp + 1, leaf] ^ 1])
                        for sp in range(6)
                    ],
                    axis=1,
                ))
            r = dot(jnp.concatenate(lhs, axis=0), blocks[t, :, q * 128:(q + 1) * 128], 1, 0)
            lanes = pl.ds(pl.multiple_of(t * 512 + q * 128, 128), 128)
            out[:, lanes] = jnp.where(mask, r[:64], r[64:])
        return carry

    lax.fori_loop(0, 8, chunk, 0, unroll=4)


def far_kernel(
    li_any, mi_any, cown, nown, ra, rb, qa, qb, za, zb, zn, far, nfar, pieces, nw, li, mi, sems
):
    loads = copies([(li_any, li), (mi_any, mi)], sems)
    mask = low_lanes(32)

    def put_leaves(nwx, nwy, k, side, first):
        for p in range(4):
            x = side[first + p * 32:first + (p + 1) * 32, :]
            at = ((nwx * 4 + nwy) * 2 + k) * 8 + 2 * p
            pieces[at] = x
            pieces[at + 1] = pltpu.roll(x.astype(F32), 64, 1).astype(BF)

    def put_nodes(nwx, nwy, side, first):
        x = side[first:first + 32, :]
        at = (nwx * 6 + nwy) * 2
        nw[at] = x
        nw[at + 1] = pltpu.roll(x.astype(F32), 64, 1).astype(BF)

    odd_c, odd_l = lax.axis_index("coarse") & 1, lax.axis_index("leaf") & 1
    in_x, in_y = ((ra, 1 - odd_c), (rb, odd_c)), ((qa, 1 - odd_l), (qb, odd_l))
    for i in range(2):
        for j in range(2):
            put_nodes(2 + i, 2 + j, nown, (i * 2 + j) * 32)
            for side, after in in_x:
                put_nodes(4 * after + i, 2 + j, side, V1 + C1 + (i * 2 + j) * 32)
            for side, after in in_y:
                first = V2 + C2 + (i * 2 + j) * 32
                put_nodes(2 + i, 4 * after + j, side, first)
                put_nodes(4 - 4 * odd_c + i, 4 * after + j, side, first + 128)
                put_nodes(4 * odd_c + i, 4 * after + j, side, first + 256)
            for k in range(2):
                put_leaves(1 + i, 1 + j, k, cown, ((i * 2 + j) * 2 + k) * 128)
    for j in range(2):
        for k in range(2):
            for side, after in in_x:
                put_leaves(3 * after, 1 + j, k, side, V1 + (2 * j + k) * 128)
    for side, after in in_y:
        for k in range(2):
            for i in range(2):
                put_leaves(1 + i, 3 * after, k, side, V2 + (2 * i + k) * 128)
            put_leaves(3 - 3 * odd_c, 3 * after, k, side, V2 + 512 + k * 128)
            put_leaves(3 * odd_c, 3 * after, k, side, V2 + 768 + k * 128)

    for c in loads:
        c.wait()
    for n in range(8):
        block = jnp.concatenate([nw[mi[n, s]] for s in range(16)], axis=0)
        nfar[n * 32:(n + 1) * 32, :] = dot(zn[n * 32:(n + 1) * 32, :], block, 1, 0)

    def leaves(t, carry):
        for u in range(4):
            n = t * 8 + 2 * u
            block = jnp.concatenate(
                [jnp.where(mask, pieces[li[s, n]], pieces[li[s, n + 1] ^ 1]) for s in range(16)],
                axis=0,
            )
            rows = pl.ds(pl.multiple_of(n * 32, 64), 64)
            r = dot(za[rows, :], block[:256], 1, 0) + dot(zb[rows, :], block[256:], 1, 0)
            far[pl.ds(pl.multiple_of(n * 32, 32), 32), :] = r[:32]
            far[pl.ds(pl.multiple_of(n * 32 + 32, 32), 32), :] = pltpu.roll(r[32:], 64, 1)
        return carry

    lax.fori_loop(0, 8, leaves, 0, unroll=8)


def table_kernel(y, received, after, own):
    half = y.shape[0]
    own[0:half, :] = y[...]
    own[half:, :] = received[...]


def down_kernel(
    dl, gl, own, other, zd, zg, dt, nt, tl, b, far, nfar, near, out_hbm, nds, out, sems
):
    cp = lax.axis_index("coarse")

    def pick(coarse, row, count):
        at = (coarse ^ cp) >> 1
        rows = pl.ds(pl.multiple_of(at * TAB + row, 16), count)
        same = ((coarse ^ cp) & 1) == 0
        return jnp.where(same, own[rows, :].astype(F32), other[rows, :].astype(F32))

    parts = []
    for s in range(8):
        x = pick(gl[0, s], 128, 16)
        parts += [x.astype(BF), pltpu.roll(x, 64, 1).astype(BF)]
    gf = dot(zg[...], jnp.concatenate(parts, axis=0), 1, 0).astype(BF)
    parts = []
    for s in range(16):
        d = dl[0, s]
        x = pick(d >> 3, ((d & 7) >> 1) * 32, 32)
        parts.append(jnp.where((d & 1) == 1, pltpu.roll(x, 64, 1), x).astype(BF))
    df = dot(zd[...], jnp.concatenate(parts, axis=0), 1, 0) + dot(dt[...], gf, 1, 0)
    nds[...] = dot(nt[...], df.astype(BF), 1, 0)
    mask = diagonal_mask()
    for n in range(8):
        nf = (nds[pl.ds(n, 32, stride=8), :] + nfar[n * 32:(n + 1) * 32, :]).astype(BF)
        rows = slice(n * 256, (n + 1) * 256)
        lf = (dot(tl[rows, :32], nf, 1, 0) + far[rows, :]).astype(BF)
        for h in range(2):
            g = 2 * n + h
            lanes = slice(g * 256, (g + 1) * 256)
            bg = b[:, lanes]
            bd = jnp.concatenate([bg, bg, bg, bg], axis=0) * mask
            x = dot(lf[h * 128:(h + 1) * 128, :64], bd, 0, 0)
            out[:, lanes] = (x + near[:, lanes]).astype(BF)
        lanes = pl.ds(n * 512, 512)
        pltpu.make_async_copy(out.at[:, lanes], out_hbm.at[:, lanes], sems.at[n]).start()
    for n in range(8):
        lanes = pl.ds(n * 512, 512)
        pltpu.make_async_copy(out.at[:, lanes], out_hbm.at[:, lanes], sems.at[n]).wait()


AN = pl.BlockSpec(memory_space=pl.ANY)
HB = pl.BlockSpec(memory_space=pltpu.HBM)
VM = pl.BlockSpec(memory_space=pltpu.VMEM)
SM = pl.BlockSpec(memory_space=pltpu.SMEM)


def shape(dims, dtype=BF):
    return jax.ShapeDtypeStruct(dims, dtype)


def params(mib):
    return pltpu.CompilerParams(vmem_limit_bytes=mib * MB)


def cost(flops, size):
    return pl.CostEstimate(flops=flops, bytes_accessed=size, transcendentals=0)


def body(
    vectors, leaf_basis, near_blocks, near_index, leaf_transfer, node_transfer, device_transfer,
    leaf_lists, leaf_coupling, node_lists, node_coupling, device_lists, device_coupling,
    group_lists, group_coupling,
):
    nt = jnp.transpose(node_transfer, (0, 2, 1)).reshape(256, 32)
    dt = device_transfer.reshape(32, 32)
    pay, cown, nown, ma, mb, tl, faces, near_ix, leaf_ix, node_ix = pl.pallas_call(
        up_kernel,
        out_shape=[
            shape((8, 32, 128)), shape((1024, 128)), shape((128, 128)),
            shape((ROWS1, 128)), shape((ROWS1, 128)), shape((2048, 128)),
            shape((1024, 128)),
            shape((12, 64), jnp.int32), shape((16, 64), jnp.int32), shape((8, 16), jnp.int32),
        ],
        in_specs=[HB] * 8,
        out_specs=[VM] * 10,
        scratch_shapes=[
            pltpu.VMEM((2048, 64), BF), pltpu.VMEM((2048, 128), F32), pltpu.VMEM((256, 128), F32),
            pltpu.VMEM((32, 32, 64), BF), pltpu.VMEM((64, 4096), BF), pltpu.VMEM((32, 4096), BF),
            pltpu.VMEM((256, 32), BF), pltpu.VMEM((32, 32), BF), pltpu.VMEM((12, 64), jnp.int32),
            pltpu.VMEM((16, 64), jnp.int32), pltpu.VMEM((8, 16), jnp.int32),
            pltpu.SemaphoreType.DMA((8,)),
        ],
        compiler_params=params(58),
        cost_estimate=cost(10**6, 10**5),
        name="up_pass",
    )(vectors, leaf_basis, leaf_transfer, nt, dt, near_index, leaf_lists, node_lists.T)

    coarse, leafs = lax.axis_size("coarse"), lax.axis_size("leaf")
    r = lax.all_to_all(pay, "leaf", 0, 0, tiled=True)

    def swap(x, axis, first):
        size = lax.axis_size(axis)
        pairs = [(i, i + 1) for i in range(first, size - 1, 2)]
        return lax.ppermute(x, axis, pairs + [(j, i) for i, j in pairs])

    ra, rb = swap(ma, "coarse", 0), swap(mb, "coarse", 1)

    half = [pltpu.VMEM((2, 2048, 128), F32), pltpu.VMEM((8, 32, 32, 64), BF)]
    za = pl.pallas_call(
        first_layout_kernel,
        out_shape=shape((2048, 256)),
        in_specs=[HB],
        out_specs=VM,
        scratch_shapes=half + [pltpu.SemaphoreType.DMA((4,))],
        compiler_params=params(50),
        cost_estimate=cost(1000, 1000000),
        name="first_layout",
    )(leaf_coupling)
    zb, zn, zd, zg = pl.pallas_call(
        second_layout_kernel,
        out_shape=[shape((2048, 256)), shape((256, 512)), shape((32, 512)), shape((32, 256))],
        in_specs=[HB] * 4,
        out_specs=[VM] * 4,
        scratch_shapes=half + [
            pltpu.VMEM((256, 128), F32), pltpu.VMEM((16, 32, 8, 32), BF),
            pltpu.VMEM((16, 32, 32), BF), pltpu.VMEM((8, 32, 32), BF),
            pltpu.SemaphoreType.DMA((4,)), pltpu.SemaphoreType.DMA((3,)),
        ],
        compiler_params=params(50),
        cost_estimate=cost(1000, 1000000),
        name="second_layout",
    )(
        leaf_coupling, jnp.transpose(node_coupling, (0, 1, 3, 2)),
        device_coupling.reshape(16, 32, 32), group_coupling.reshape(8, 32, 32),
    )

    sa, sb = pl.pallas_call(
        pack_kernel,
        out_shape=[shape((ROWS2, 128))] * 2,
        in_specs=[VM] * 5,
        out_specs=[VM] * 2,
        compiler_params=params(8),
        cost_estimate=cost(1000, 10000000),
        name="halo_pack",
    )(faces, cown, nown, ra, rb)
    qa, qb = swap(sa, "leaf", 0), swap(sb, "leaf", 1)

    y = pl.pallas_call(
        group_kernel,
        out_shape=shape((TAB, 128)),
        in_specs=[VM, AN],
        out_specs=VM,
        compiler_params=params(8),
        cost_estimate=cost(1000, 10**5),
        name="group_sum",
    )(r, za)
    flip = lambda x, bit: lax.ppermute(x, "coarse", [(i, i ^ bit) for i in range(coarse)])

    def join(first, second, after):
        return pl.pallas_call(
            table_kernel,
            out_shape=shape((2 * first.shape[0], 128)),
            in_specs=[VM, VM, AN],
            out_specs=VM,
            compiler_params=params(8),
            cost_estimate=cost(1000, 10**5),
            name="table_join",
        )(first, second, after)


    y = join(y, flip(y, 2), sa)
    y = jnp.concatenate([y, flip(y, 4)], axis=0)
    received = flip(y, 8)

    near = pl.pallas_call(
        near_kernel,
        out_shape=shape((64, 4096), F32),
        in_specs=[AN, VM, VM, VM, VM, VM, HB],
        out_specs=VM,
        scratch_shapes=[
            pltpu.VMEM((144, 64, 128), BF), pltpu.SMEM((12, 64), jnp.int32),
            pltpu.VMEM((8, 768, 512), BF), pltpu.SemaphoreType.DMA((9,)),
        ],
        compiler_params=params(48),
        cost_estimate=cost(1000, 1000000),
        name="near_field",
    )(near_ix, vectors, ra, rb, qa, qb, near_blocks.reshape(768, 4096))


    y = join(y, received, zn)
    received = flip(y, 16)

    far, nfar = pl.pallas_call(
        far_kernel,
        out_shape=[shape((2048, 128), F32), shape((256, 128), F32)],
        in_specs=[AN] * 2 + [VM] * 9,
        out_specs=[VM] * 2,
        scratch_shapes=[
            pltpu.VMEM((256, 32, 128), BF), pltpu.VMEM((72, 32, 128), BF), pltpu.SMEM((16, 64), jnp.int32), pltpu.SMEM((8, 16), jnp.int32),
            pltpu.SemaphoreType.DMA((2,)),
        ],
        compiler_params=params(32),
        cost_estimate=cost(1000, 1000000),
        name="far_field",
    )(leaf_ix, node_ix, cown, nown, ra, rb, qa, qb, za, zb, zn)

    own = join(y, received, near)
    other = flip(own, 1)

    return pl.pallas_call(
        down_kernel,
        out_shape=shape((64, 4096)),
        in_specs=[SM] * 2 + [VM] * 11,
        out_specs=HB,
        scratch_shapes=[
            pltpu.VMEM((256, 128), F32), pltpu.VMEM((64, 4096), BF), pltpu.SemaphoreType.DMA((8,)),
        ],
        compiler_params=params(32),
        cost_estimate=cost(10**6, 10**5),
        name="down_pass",
    )(
        device_lists.reshape(1, 16), group_lists.reshape(1, 8), own, other, zd, zg, dt, nt, tl,
        leaf_basis, far, nfar, near,
    )


def solution(mesh):
    both = ("coarse", "leaf")
    placed = (
        P(None, both), P(None, both), P(None, None, both), P(None, both), P(None, None, both),
        P(None, None, both), P(None, None, both), P(None, both), P(None, None, None, both),
        P(None, both), P(None, None, None, both), P(None, both), P(None, None, None, both),
        P(None, "coarse"), P(None, None, None, "coarse"),
    )
    return jax.shard_map(
        body, mesh=mesh, in_specs=placed, out_specs=P(None, both), check_vma=False
    )
```
